32 devices in a mesh: seq: 8 (over y, x, core), head: 4 (over z).
Axes of the slice: x: 2, y: 2, z: 4, core: 2. Of those that a mesh axis runs over, the one named last changes fastest.
Arguments:
- queries: bfloat16 [1024, 6144], P('seq', 'head'), may hold values from -60 to 60
- keys: bfloat16 [1024, 6144], P('seq', 'head'), may hold values from -6 to 6
- values: bfloat16 [1024, 6144], P('seq', 'head'), may hold values from -6 to 6
- band: int32 [48], P('head'), may hold values from 16 to 64
- picks: int32 [8, 16], P('seq'), may hold values from 0 to 127, as said below
- w_out: bfloat16 [6144, 6144], P('seq', 'head'), may hold values from -0.078125 to 0.078125
Outputs:
- output: bfloat16 [1024, 6144], P(('seq', 'head'))
The draws below stay inside these ranges and needn't reach their ends.
Inputs may be any that keep to these rules, and one draw needn't show every extreme that they name: The 16 entries of a row of picks are distinct.
All inputs are finite; a program needn't handle non-finite values.
Results may differ from the reference program's by a relative error of at most 0.015.
Values may be sent and summed in bfloat16 or wider, within the bound.
No kernel may reach another device: no remote copies, remote signals or barrier semaphores. Data moves between devices by JAX's collectives and lax.ppermute only.
A program may use at most 128 MiB of HBM per device.

```python
import math
import jax
import jax.numpy as jnp
from jax import lax

HEADS = 48
HD = 128
DW = 6144
BLOCK = 128
SUMS = 16
TOKENS = 1024
NBLOCKS = 8
FEAT = 6144


def key_field(key):
    base = jax.random.fold_in(key, 7)
    field = jnp.clip(jax.random.normal(base, (TOKENS, FEAT), jnp.float32), -6.0, 6.0)
    return field


def draw_queries(key, part):
    other = jax.random.fold_in(key, 8)
    return (3.0 * jnp.clip(jax.random.normal(other, (TOKENS, FEAT), jnp.float32), -6.0, 6.0)).astype(jnp.bfloat16)


def draw_keys(key, part):
    field = key_field(key)
    return field.astype(jnp.bfloat16)


def draw_band(key, part):
    lowest = max(2, BLOCK // 8)
    highest = BLOCK // 2
    widths = jax.random.randint(jax.random.fold_in(key, 3), (HEADS,), lowest, highest + 1)
    order = jax.random.permutation(jax.random.fold_in(key, 4), HEADS)
    widths = widths.at[order[0]].set(highest)
    widths = widths.at[order[1]].set(lowest)
    return widths.astype(jnp.int32)


def draw_picks(key, part):
    raw = jax.random.randint(jax.random.fold_in(key, 5), (NBLOCKS, BLOCK), 0, 1 << 20)
    scores = raw * BLOCK + jnp.arange(BLOCK, dtype=jnp.int32)[None, :]
    unused, chosen = lax.top_k(scores, SUMS)
    return chosen.astype(jnp.int32)


def levels(rng, shape, shards, least, high):
    level, own = 1.0, jax.random.fold_in(rng, 6)
    for dim, parts in shards:
        steps = jnp.exp(jax.random.uniform(jax.random.fold_in(own, dim), (parts,), jnp.float32, least / len(shards), high / len(shards)))
        level = level * jnp.repeat(steps, shape[dim] // parts).reshape([-1 if axis == dim else 1 for axis in range(len(shape))])
    return level


def bell_draw(own_key, shape, scale, limit, shards=(), held_as=jnp.bfloat16):
    loudness = levels(own_key, shape, shards, -0.22, 0.18) if shards else 1.0
    entries = jax.random.normal(own_key, shape, jnp.float32) * scale * loudness
    return jnp.minimum(jnp.maximum(entries, -limit), limit).astype(held_as)


def setup_inputs(seed: int = 0) -> dict:
    key_of = jax.random.split(jax.random.key(seed), 7)
    return {
        "queries": draw_queries(jax.random.fold_in(key_of[6], 71), 0),
        "keys": draw_keys(jax.random.fold_in(key_of[6], 71), 0),
        "values": bell_draw(key_of[2], (TOKENS, FEAT), 1.0, 6.0, ((0, 8), (1, 4))),
        "band": draw_band(jax.random.fold_in(key_of[6], 71), 0),
        "picks": draw_picks(jax.random.fold_in(key_of[6], 71), 0),
        "w_out": bell_draw(key_of[5], (DW, FEAT), FEAT ** -0.5, 0.078125, ((0, 8), (1, 4))),
    }


NEGATIVE_FILL = -1e+30

def reference(queries, keys, values, band, picks, w_out):
    count = TOKENS // BLOCK
    shape_four = (count, BLOCK, HEADS, HD)
    query_blocks = queries.reshape(shape_four)
    key_blocks = keys.reshape(shape_four)
    value_blocks = values.reshape(shape_four)
    chosen = picks[:, :, None, None]
    summary_keys = jnp.take_along_axis(key_blocks, chosen, axis=1).reshape(count * SUMS, HEADS, HD).astype(jnp.float32)
    summary_values = jnp.take_along_axis(value_blocks, chosen, axis=1).reshape(count * SUMS, HEADS, HD).astype(jnp.float32)
    owner = jnp.arange(count * SUMS, dtype=jnp.int32) // SUMS
    zero_block = jnp.zeros((1, BLOCK, HEADS, HD), keys.dtype)
    prior_keys = jnp.concatenate([zero_block, key_blocks[:-1]], 0)
    prior_values = jnp.concatenate([zero_block, value_blocks[:-1]], 0)
    scale = 1.0 / math.sqrt(HD)

    def one_block(item):
        number, query, own_keys, own_values, back_keys, back_values = item
        window_keys = jnp.concatenate([back_keys, own_keys], 0).astype(jnp.float32)
        window_values = jnp.concatenate([back_values, own_values], 0).astype(jnp.float32)
        query_wide = query.astype(jnp.float32)
        near = jnp.einsum('uhd,thd->hut', query_wide, window_keys) * scale
        query_pos = number * BLOCK + jnp.arange(BLOCK, dtype=jnp.int32)
        key_pos = number * BLOCK - BLOCK + jnp.arange(2 * BLOCK, dtype=jnp.int32)
        key_grid = key_pos[None, None, :]
        query_grid = query_pos[None, :, None]
        near_ok = (key_grid <= query_grid) & (key_grid > query_grid - band[:, None, None]) & (key_grid >= 0)
        far = jnp.einsum('uhd,shd->hus', query_wide, summary_keys) * scale
        far_ok = jnp.broadcast_to((owner < number)[None, None, :], far.shape)
        valid = jnp.concatenate([near_ok, far_ok], -1)
        scores = jnp.concatenate([near, far], -1)
        scores = jnp.where(valid, scores, NEGATIVE_FILL)
        largest = lax.optimization_barrier(jnp.max(scores, axis=-1, keepdims=True))
        weights = jnp.where(valid, jnp.exp(scores - largest), 0.0)
        total = lax.optimization_barrier(jnp.sum(weights, axis=-1, keepdims=True))
        rounded = lax.optimization_barrier(weights.astype(jnp.bfloat16)).astype(jnp.float32)
        both_values = jnp.concatenate([window_values, summary_values], 0)
        mixed = jnp.einsum('hut,thd->hud', rounded, both_values) / total
        return mixed.transpose(1, 0, 2).reshape(BLOCK, HEADS * HD).astype(jnp.bfloat16)
    numbers = jnp.arange(count, dtype=jnp.int32)
    attention = lax.map(one_block, (numbers, query_blocks, key_blocks, value_blocks, prior_keys, prior_values))
    attention = attention.reshape(TOKENS, HEADS * HD)
    return jnp.dot(attention, w_out.T, preferred_element_type=jnp.float32).astype(jnp.bfloat16)
```

```python
import math

import jax
import jax.numpy as jnp
from jax import lax
from jax.experimental import pallas as pl
from jax.experimental.pallas import tpu as pltpu
from jax.sharding import PartitionSpec as P

BLOCK = 128
HALO = 64
NEGATIVE_FILL = -1e30
LAST = (((1,), (1,)), ((), ()))


def vmem():
    return pl.BlockSpec(memory_space=pltpu.VMEM)


def smem():
    return pl.BlockSpec(memory_space=pltpu.SMEM)


def pick_kernel(picks_ref, keys_ref, values_ref, summary_ref, halo_ref):
    per_block = picks_ref.shape[1]
    row = lax.broadcasted_iota(jnp.int32, (per_block, BLOCK), 0)
    wanted = jnp.zeros((per_block, BLOCK), jnp.int32)
    for r in range(per_block):
        wanted = jnp.where(row == r, picks_ref[0, r], wanted)
    column = lax.broadcasted_iota(jnp.int32, (per_block, BLOCK), 1)
    chosen = jnp.where(column == wanted, 1.0, 0.0).astype(jnp.bfloat16)
    for part, ref in enumerate((keys_ref, values_ref)):
        taken = jnp.dot(chosen, ref[...], preferred_element_type=jnp.float32)
        summary_ref[part] = taken.astype(jnp.bfloat16)
        halo_ref[part] = ref[BLOCK - HALO :, :]


def attend_kernel(band_ref, q_ref, k_ref, v_ref, halo_ref, far_ref, out_ref):
    heads = band_ref.shape[0]
    size = q_ref.shape[1] // heads
    sources, unused, per_block, feat = far_ref.shape
    far_rows = sources * per_block
    place = lax.axis_index("seq")
    scale = 1.0 / math.sqrt(size)
    own_q = lax.broadcasted_iota(jnp.int32, (BLOCK, BLOCK), 0)
    own_k = lax.broadcasted_iota(jnp.int32, (BLOCK, BLOCK), 1)
    own_gap = own_q - own_k
    back_q = lax.broadcasted_iota(jnp.int32, (BLOCK, HALO), 0)
    back_k = lax.broadcasted_iota(jnp.int32, (BLOCK, HALO), 1) - HALO
    back_gap = jnp.where(place > 0, back_q - back_k, BLOCK * 4)
    far_owner = lax.broadcasted_iota(jnp.int32, (BLOCK, far_rows), 1) // per_block
    far_ok = far_owner < place
    for h in range(heads):
        cols = slice(h * size, (h + 1) * size)
        query = q_ref[:, cols]
        all_keys = jnp.concatenate(
            [k_ref[:, cols], far_ref[:, 0, :, cols].reshape(far_rows, size), halo_ref[0, :, cols]], 0
        )
        all_values = jnp.concatenate(
            [v_ref[:, cols], far_ref[:, 1, :, cols].reshape(far_rows, size), halo_ref[1, :, cols]], 0
        )
        scores = lax.dot_general(query, all_keys, LAST, preferred_element_type=jnp.float32) * scale
        own_ok = (own_gap >= 0) & (own_gap < band_ref[h])
        back_ok = back_gap < band_ref[h]
        valid = jnp.concatenate([own_ok, far_ok, back_ok], 1)
        scores = jnp.where(valid, scores, NEGATIVE_FILL)
        largest = jnp.max(scores, axis=1, keepdims=True)
        weights = jnp.where(valid, jnp.exp(scores - largest), 0.0)
        total = jnp.sum(weights, axis=1, keepdims=True)
        mixed = jnp.dot(weights.astype(jnp.bfloat16), all_values, preferred_element_type=jnp.float32)
        out_ref[:, cols] = (mixed / total).astype(jnp.bfloat16)


def project_kernel(att_ref, w_ref, out_ref):
    parts, unused, rows, wide = out_ref.shape
    found = lax.dot_general(att_ref[...], w_ref[...], LAST, preferred_element_type=jnp.float32)
    out_ref[...] = found.astype(jnp.bfloat16).reshape(parts, 1, rows, wide)


def local(queries, keys, values, band, picks, w_out):
    heads = band.shape[0]
    tok_rows, feat = queries.shape
    per_block = picks.shape[1]
    seq = lax.axis_size("seq")
    groups = lax.axis_size("head")
    wide = w_out.shape[0]
    rows = tok_rows // groups
    bf16 = jnp.bfloat16
    summary, halo = pl.pallas_call(
        pick_kernel,
        out_shape=(
            jax.ShapeDtypeStruct((2, per_block, feat), bf16),
            jax.ShapeDtypeStruct((2, HALO, feat), bf16),
        ),
        in_specs=[smem(), vmem(), vmem()],
        out_specs=(vmem(), vmem()),
    )(picks, keys, values)
    far = lax.all_gather(summary, "seq", axis=0, tiled=False)
    halo = lax.ppermute(halo, "seq", [(i, i + 1) for i in range(seq - 1)])
    attention = pl.pallas_call(
        attend_kernel,
        out_shape=jax.ShapeDtypeStruct((tok_rows, feat), bf16),
        in_specs=[smem()] + [vmem()] * 5,
        out_specs=vmem(),
        compiler_params=pltpu.CompilerParams(vmem_limit_bytes=40 << 20),
    )(band, queries, keys, values, halo, far)
    gathered = lax.all_gather(attention, "seq", axis=0, tiled=True)
    partial_value = pl.pallas_call(
        project_kernel,
        grid=(seq,),
        out_shape=jax.ShapeDtypeStruct((groups, seq, rows, wide), bf16),
        in_specs=[
            pl.BlockSpec((tok_rows, feat), lambda s: (s, 0)),
            pl.BlockSpec((wide, feat), lambda s: (0, 0)),
        ],
        out_specs=pl.BlockSpec((groups, 1, rows, wide), lambda s: (0, s, 0, 0)),
        compiler_params=pltpu.CompilerParams(vmem_limit_bytes=40 << 20),
    )(gathered, w_out)
    summed = lax.psum_scatter(
        partial_value.reshape(groups * seq * rows, wide), "head", scatter_dimension=0, tiled=True
    )
    moved = lax.all_to_all(summed.reshape(seq, rows, wide), "seq", 0, 0, tiled=False)
    return moved.transpose(1, 0, 2).reshape(rows, seq * wide)


def solution(mesh):
    placed = (
        P("seq", "head"),
        P("seq", "head"),
        P("seq", "head"),
        P("head"),
        P("seq", None),
        P("seq", "head"),
    )
    return jax.shard_map(
        local, mesh=mesh, in_specs=placed, out_specs=P(("seq", "head"), None), check_vma=False
    )
```

```python
import math

import jax
import jax.numpy as jnp
from jax import lax
from jax.experimental import pallas as pl
from jax.experimental.pallas import tpu as pltpu
from jax.sharding import PartitionSpec as P

BLOCK = 128
HALO = 64
NEGATIVE_FILL = -1e30
LAST = (((1,), (1,)), ((), ()))
BF16 = jnp.bfloat16
PARAMS = pltpu.CompilerParams(vmem_limit_bytes=40 << 20)
WHOLE = pltpu.CompilerParams(vmem_limit_bytes=62 << 20)


def vmem():
    return pl.BlockSpec(memory_space=pltpu.VMEM)


def smem():
    return pl.BlockSpec(memory_space=pltpu.SMEM)


def hbm():
    return pl.BlockSpec(memory_space=pltpu.HBM)


def shaped(*shape):
    return jax.ShapeDtypeStruct(shape, BF16)


def pick_kernel(picks_ref, keys_ref, values_ref, summary_ref, halo_ref, rows_ref, sems):
    per_block = picks_ref.shape[1]
    copies = [
        pltpu.make_async_copy(ref, rows_ref.at[part], sems.at[part])
        for part, ref in enumerate((keys_ref, values_ref))
    ]
    for copy in copies:
        copy.start()
    row = lax.broadcasted_iota(jnp.int32, (per_block, BLOCK), 0)
    wanted = jnp.zeros((per_block, BLOCK), jnp.int32)
    for r in range(per_block):
        wanted = jnp.where(row == r, picks_ref[0, r], wanted)
    column = lax.broadcasted_iota(jnp.int32, (per_block, BLOCK), 1)
    chosen = jnp.where(column == wanted, 1.0, 0.0).astype(BF16)
    for part, copy in enumerate(copies):
        copy.wait()
        taken = jnp.dot(chosen, rows_ref[part], preferred_element_type=jnp.float32)
        summary_ref[part] = taken.astype(BF16)
        halo_ref[part] = rows_ref[part, BLOCK - HALO :, :]


def attend_kernel(band_ref, q_hbm, k_hbm, v_hbm, halo_ref, far_ref, out_ref, q_ref, k_ref, v_ref, sems):
    size = BLOCK
    feat = q_ref.shape[1]
    heads = feat // size
    sources, unused, per_block, unused = far_ref.shape
    far_rows = sources * per_block
    some = 3 if heads % 3 == 0 else 1
    span = some * size
    copies = []
    for g in range(heads // some):
        cols = slice(g * span, (g + 1) * span)
        copies.append(
            [
                pltpu.make_async_copy(ref.at[:, cols], into.at[:, cols], sems.at[g, part])
                for part, (ref, into) in enumerate(((q_hbm, q_ref), (k_hbm, k_ref), (v_hbm, v_ref)))
            ]
        )
        for copy in copies[-1]:
            copy.start()
    place = lax.axis_index("seq")
    scale = 1.0 / math.sqrt(size)
    own_q = lax.broadcasted_iota(jnp.int32, (BLOCK, BLOCK), 0)
    own_k = lax.broadcasted_iota(jnp.int32, (BLOCK, BLOCK), 1)
    own_gap = own_q - own_k
    back_q = lax.broadcasted_iota(jnp.int32, (BLOCK, HALO), 0)
    back_k = lax.broadcasted_iota(jnp.int32, (BLOCK, HALO), 1) - HALO
    back_gap = jnp.where(place > 0, back_q - back_k, BLOCK * 4)
    far_owner = lax.broadcasted_iota(jnp.int32, (BLOCK, far_rows), 1) // per_block
    far_ok = far_owner < place
    for h in range(heads):
        if h % some == 0:
            for copy in copies[h // some]:
                copy.wait()
        cols = slice(h * size, (h + 1) * size)
        query = q_ref[:, cols]
        all_keys = jnp.concatenate(
            [k_ref[:, cols], far_ref[:, 0, :, cols].reshape(far_rows, size), halo_ref[0, :, cols]], 0
        )
        all_values = jnp.concatenate(
            [v_ref[:, cols], far_ref[:, 1, :, cols].reshape(far_rows, size), halo_ref[1, :, cols]], 0
        )
        scores = lax.dot_general(query, all_keys, LAST, preferred_element_type=jnp.float32) * scale
        width = band_ref[h]
        own_ok = (own_gap >= 0) & (own_gap < width)
        back_ok = back_gap < width
        valid = jnp.concatenate([own_ok, far_ok, back_ok], 1)
        scores = jnp.where(valid, scores, NEGATIVE_FILL)
        largest = jnp.max(scores, axis=1, keepdims=True)
        weights = jnp.where(valid, jnp.exp(scores - largest), 0.0)
        total = jnp.sum(weights, axis=1, keepdims=True)
        mixed = jnp.dot(weights.astype(BF16), all_values, preferred_element_type=jnp.float32)
        out_ref[:, cols] = (mixed / total).astype(BF16)


def project_kernel(att_ref, mine_ref, other_ref, *refs):
    send_ref, keep_ref, acc_ref = refs[-3:]
    wide = mine_ref.shape[0]
    unused, half, rows, unused = keep_ref.shape
    core = lax.rem(lax.axis_index("seq"), 2)
    side = lax.rem(lax.axis_index("head"), 2)
    step = acc_ref.shape[-1]
    for which, ref in ((core, mine_ref), (1 - core, other_ref)):

        @pl.loop(0, wide // step)
        def _(n):
            tile = ref[pl.ds(n * step, step), :]
            found = lax.dot_general(att_ref[...], tile, LAST, preferred_element_type=jnp.float32)
            acc_ref[...] = found.reshape(half, 2, rows, step)
            cols = slice(None) if step == wide else pl.ds(pl.multiple_of(n * step, step), step)
            keep_ref[which, :, :, cols] = acc_ref[:, side].astype(BF16)
            send_ref[which, :, :, cols] = acc_ref[:, 1 - side].astype(BF16)


def split_kernel(came_ref, keep_ref, away_ref, stay_ref):
    side = lax.axis_index("head") // 2
    for ref, which in ((away_ref, 1 - side), (stay_ref, side)):
        total = came_ref[:, which].astype(jnp.float32) + keep_ref[:, which].astype(jnp.float32)
        ref[...] = total.astype(BF16)


def join_kernel(*refs):
    out_ref = refs[-1]
    wide = refs[0].shape[-1]
    chip = lax.axis_index("seq") // 2
    for k in range(len(refs) // 2):
        total = refs[2 * k][...].astype(jnp.float32) + refs[2 * k + 1][...].astype(jnp.float32)
        total = total.astype(BF16)
        if len(out_ref.shape) == 4:
            out_ref[chip ^ k] = total
            continue
        for c in range(2):
            start = pl.multiple_of((chip ^ k) * (2 * wide), 128)
            out_ref[:, pl.ds(start + c * wide, wide)] = total[c]


def local(queries, keys, values, band, picks, w_out):
    heads = band.shape[0]
    tok_rows, feat = queries.shape
    per_block = picks.shape[1]
    seq = lax.axis_size("seq")
    groups = lax.axis_size("head")
    wide = w_out.shape[0]
    rows = tok_rows // groups
    chips = seq // 2
    half = groups // 2

    def swap(value, k, z):
        if k == 0:
            return lax.ppermute(value, "head", [(i, i ^ z) for i in range(groups)])
        if z == 0:
            return lax.ppermute(value, "seq", [(i, i ^ k) for i in range(seq)])
        pairs = [
            (s * groups + h, (s ^ k) * groups + (h ^ z)) for s in range(seq) for h in range(groups)
        ]
        return lax.ppermute(value, ("seq", "head"), pairs)

    summary, halo = pl.pallas_call(
        pick_kernel,
        out_shape=(shaped(2, per_block, feat), shaped(2, HALO, feat)),
        in_specs=[smem(), hbm(), hbm()],
        out_specs=(vmem(), vmem()),
        scratch_shapes=[pltpu.VMEM((2, tok_rows, feat), BF16), pltpu.SemaphoreType.DMA((2,))],
        compiler_params=WHOLE,
    )(picks, keys, values)
    halo = lax.ppermute(halo, "seq", [(i, i + 1) for i in range(seq - 1)])
    other_w = swap(w_out, 1, 0)
    far = lax.all_gather(summary, "seq", axis=0, tiled=False)
    attention = pl.pallas_call(
        attend_kernel,
        out_shape=shaped(tok_rows, feat),
        in_specs=[smem(), hbm(), hbm(), hbm(), vmem(), vmem()],
        out_specs=vmem(),
        scratch_shapes=[pltpu.VMEM((tok_rows, feat), BF16)] * 3 + [pltpu.SemaphoreType.DMA((heads, 3))],
        compiler_params=WHOLE,
    )(band, queries, keys, values, halo, far)
    step = 256 if wide % 256 == 0 else wide
    pieces = []
    before = ()
    for k in range(chips):
        part = swap(attention, 2 * k, 0) if k else attention
        send, keep = pl.pallas_call(
            project_kernel,
            out_shape=(shaped(2, half, rows, wide), shaped(2, half, rows, wide)),
            in_specs=[vmem()] * 3 + [pl.BlockSpec(memory_space=pl.ANY)] * len(before),
            out_specs=(vmem(), vmem()),
            scratch_shapes=[pltpu.VMEM((half, 2, rows, step), jnp.float32)],
            compiler_params=PARAMS,
        )(part, w_out, other_w, *before)
        before = (send,)
        came = swap(send, 0, 1)
        away, stay = pl.pallas_call(
            split_kernel,
            out_shape=(shaped(2, rows, wide), shaped(2, rows, wide)),
            in_specs=[vmem()] * 2,
            out_specs=(vmem(), vmem()),
        )(came, keep)
        pieces.append(swap(away, 2 * k, 2))
        pieces.append(swap(stay, 2 * k, 0) if k else stay)
    flat = wide % 128 == 0
    joined = pl.pallas_call(
        join_kernel,
        out_shape=shaped(rows, seq * wide) if flat else shaped(chips, 2, rows, wide),
        in_specs=[vmem()] * len(pieces),
        out_specs=vmem(),
        compiler_params=PARAMS,
    )(*pieces)
    return joined if flat else joined.transpose(2, 0, 1, 3).reshape(rows, seq * wide)


def solution(mesh):
    placed = (
        P("seq", "head"),
        P("seq", "head"),
        P("seq", "head"),
        P("head"),
        P("seq", None),
        P("seq", "head"),
    )
    return jax.shard_map(
        local, mesh=mesh, in_specs=placed, out_specs=P(("seq", "head"), None), check_vma=False
    )
```

```python
import math

import jax
import jax.numpy as jnp
from jax import lax
from jax.experimental import pallas as pl
from jax.experimental.pallas import tpu as pltpu
from jax.sharding import PartitionSpec as P

BLOCK = 128
HALO = 64
NEGATIVE_FILL = -1e30
LAST = (((1,), (1,)), ((), ()))
BF16 = jnp.bfloat16
PARAMS = pltpu.CompilerParams(vmem_limit_bytes=32 << 20)


def vmem():
    return pl.BlockSpec(memory_space=pltpu.VMEM)


def smem():
    return pl.BlockSpec(memory_space=pltpu.SMEM)


def hbm():
    return pl.BlockSpec(memory_space=pltpu.HBM)


def shaped(*shape):
    return pltpu.VMEM(shape, BF16)


def far_away(*arrays):
    return [pltpu.with_memory_space_constraint(array, pltpu.HBM) for array in arrays]


def column_of(count, width, number):
    row = lax.broadcasted_iota(jnp.int32, (count, width), 0)
    found = jnp.zeros((count, width), jnp.int32)
    for r in range(count):
        found = jnp.where(row == r, number(r), found)
    return found


def pick_kernel(
    picks_ref, band_ref, q_hbm, k_hbm, v_hbm, summary_ref, halo_ref, width_ref, q_ref, k_ref, v_ref, sems
):
    per_block = picks_ref.shape[1]
    copies = [
        pltpu.make_async_copy(ref, into, sems.at[part])
        for part, (ref, into) in enumerate(((k_hbm, k_ref), (v_hbm, v_ref), (q_hbm, q_ref)))
    ]
    for copy in copies:
        copy.start()
    wanted = column_of(per_block, BLOCK, lambda r: picks_ref[0, r])
    width_ref[...] = column_of(*width_ref.shape, lambda r: band_ref[r])
    column = lax.broadcasted_iota(jnp.int32, (per_block, BLOCK), 1)
    chosen = jnp.where(column == wanted, 1.0, 0.0).astype(BF16)
    for part, ref in enumerate((k_ref, v_ref)):
        copies[part].wait()
        taken = jnp.dot(chosen, ref[...], preferred_element_type=jnp.float32)
        summary_ref[part] = taken.astype(BF16)
        halo_ref[part] = ref[BLOCK - HALO :, :]
    copies[2].wait()


def stack_kernel(*refs):
    for k, ref in enumerate(refs[:-1]):
        refs[-1][k] = ref[...]


def attend_kernel(width_ref, q_ref, k_ref, v_ref, halo_ref, mine_ref, other_ref, out_ref):
    size = BLOCK
    heads = q_ref.shape[1] // size
    chips, unused, per_block, unused = mine_ref.shape
    far_rows = chips * per_block
    place = lax.axis_index("seq")
    chip = place // 2
    core = lax.rem(place, 2)
    scale = 1.0 / math.sqrt(size)
    never = 4 * BLOCK
    own_gap = lax.broadcasted_iota(jnp.int32, (BLOCK, BLOCK), 0) - lax.broadcasted_iota(
        jnp.int32, (BLOCK, BLOCK), 1
    )
    own_gap = jnp.where(own_gap >= 0, own_gap, never)
    back_gap = lax.broadcasted_iota(jnp.int32, (BLOCK, HALO), 0) - lax.broadcasted_iota(
        jnp.int32, (BLOCK, HALO), 1
    )
    back_gap = jnp.where(place > 0, back_gap + HALO, never)
    far_chip = (lax.broadcasted_iota(jnp.int32, (BLOCK, far_rows), 1) // per_block) ^ chip
    mine_gap = jnp.where(far_chip * 2 + core < place, 0, never)
    other_gap = jnp.where(far_chip * 2 + (1 - core) < place, 0, never)
    gap = jnp.concatenate([own_gap, mine_gap, other_gap, back_gap], 1)
    for h in range(heads):
        cols = slice(h * size, (h + 1) * size)
        query = q_ref[:, cols]
        joined = [
            jnp.concatenate(
                [
                    own[:, cols],
                    mine_ref[:, part, :, cols].reshape(far_rows, size),
                    other_ref[:, part, :, cols].reshape(far_rows, size),
                    halo_ref[part, :, cols],
                ],
                0,
            )
            for part, own in enumerate((k_ref, v_ref))
        ]
        scores = lax.dot_general(query, joined[0], LAST, preferred_element_type=jnp.float32) * scale
        valid = gap < width_ref[h : h + 1, :]
        scores = jnp.where(valid, scores, NEGATIVE_FILL)
        largest = jnp.max(scores, axis=1, keepdims=True)
        weights = jnp.where(valid, jnp.exp(scores - largest), 0.0)
        total = jnp.sum(weights, axis=1, keepdims=True)
        mixed = jnp.dot(weights.astype(BF16), joined[1], preferred_element_type=jnp.float32)
        out_ref[:, cols] = (mixed / total).astype(BF16)


def project_kernel(att_ref, mine_ref, other_ref, *refs):
    send_ref, keep_ref = refs[-2:]
    half, unused, rows, feat = att_ref.shape
    count = half * rows
    core = lax.rem(lax.axis_index("seq"), 2)
    side = lax.rem(lax.axis_index("head"), 2)
    rows_in = jnp.concatenate(
        [att_ref[:, 1 - side].reshape(count, feat), att_ref[:, side].reshape(count, feat)], 0
    )
    for which, ref in ((core, mine_ref), (1 - core, other_ref)):
        found = lax.dot_general(rows_in, ref[...], LAST, preferred_element_type=jnp.float32)
        found = found.astype(BF16).reshape(2, half, rows, ref.shape[0])
        send_ref[which] = found[0]
        keep_ref[which] = found[1]


def split_kernel(came_ref, keep_ref, away_ref, stay_ref):
    side = lax.axis_index("head") // 2
    for ref, which in ((away_ref, 1 - side), (stay_ref, side)):
        total = came_ref[:, which].astype(jnp.float32) + keep_ref[:, which].astype(jnp.float32)
        ref[...] = total.astype(BF16)


def join_kernel(*refs):
    out_ref = refs[-1]
    wide = refs[0].shape[-1]
    chip = lax.axis_index("seq") // 2
    for k in range(len(refs) // 2):
        total = refs[2 * k][...].astype(jnp.float32) + refs[2 * k + 1][...].astype(jnp.float32)
        total = total.astype(BF16)
        if len(out_ref.shape) == 4:
            out_ref[chip ^ k] = total
            continue
        for c in range(2):
            start = pl.multiple_of((chip ^ k) * (2 * wide), 128)
            out_ref[:, pl.ds(start + c * wide, wide)] = total[c]


def local(queries, keys, values, band, picks, w_out):
    heads = band.shape[0]
    tok_rows, feat = queries.shape
    per_block = picks.shape[1]
    seq = lax.axis_size("seq")
    groups = lax.axis_size("head")
    wide = w_out.shape[0]
    rows = tok_rows // groups
    chips = seq // 2
    half = groups // 2

    def swap(value, k, z):
        if k == 0:
            return lax.ppermute(value, "head", [(i, i ^ z) for i in range(groups)])
        if z == 0:
            return lax.ppermute(value, "seq", [(i, i ^ k) for i in range(seq)])
        pairs = [
            (s * groups + h, (s ^ k) * groups + (h ^ z)) for s in range(seq) for h in range(groups)
        ]
        return lax.ppermute(value, ("seq", "head"), pairs)

    other_w = swap(w_out, 1, 0)
    listed = BLOCK + HALO + seq * per_block
    summary, halo, width, queries, keys, values = pl.pallas_call(
        pick_kernel,
        out_shape=(
            shaped(2, per_block, feat),
            shaped(2, HALO, feat),
            pltpu.VMEM((heads, listed), jnp.int32),
        )
        + (shaped(tok_rows, feat),) * 3,
        in_specs=[smem(), smem(), hbm(), hbm(), hbm()],
        out_specs=(vmem(),) * 6,
        scratch_shapes=[pltpu.SemaphoreType.DMA((3,))],
        compiler_params=PARAMS,
    )(*far_away(picks, band, queries, keys, values))
    far = [summary] + [swap(summary, 2 * k, 0) for k in range(1, chips)]
    halo = lax.ppermute(halo, "seq", [(i, i + 1) for i in range(seq - 1)])
    mine = pl.pallas_call(
        stack_kernel,
        out_shape=shaped(chips, 2, per_block, feat),
        in_specs=[vmem()] * chips,
        out_specs=vmem(),
        compiler_params=PARAMS,
    )(*far)
    other = swap(mine, 1, 0)
    attention = pl.pallas_call(
        attend_kernel,
        out_shape=shaped(tok_rows, feat),
        in_specs=[vmem()] * 7,
        out_specs=vmem(),
        compiler_params=PARAMS,
    )(width, queries, keys, values, halo, mine, other)
    pieces = []
    before = ()
    for k in range(chips):
        part = swap(attention, 2 * k, 0) if k else attention
        send, keep = pl.pallas_call(
            project_kernel,
            out_shape=(shaped(2, half, rows, wide), shaped(2, half, rows, wide)),
            in_specs=[vmem()] * 3 + [pl.BlockSpec(memory_space=pl.ANY)] * len(before),
            out_specs=(vmem(), vmem()),
            compiler_params=PARAMS,
        )(part.reshape(half, 2, rows, feat), w_out, other_w, *before)
        before = (send,)
        came = swap(send, 0, 1)
        away, stay = pl.pallas_call(
            split_kernel,
            out_shape=(shaped(2, rows, wide), shaped(2, rows, wide)),
            in_specs=[vmem()] * 2,
            out_specs=(vmem(), vmem()),
            compiler_params=PARAMS,
        )(came, keep)
        pieces.append(swap(away, 2 * k, 2))
        pieces.append(swap(stay, 2 * k, 0) if k else stay)
    flat = wide % 128 == 0
    joined = pl.pallas_call(
        join_kernel,
        out_shape=jax.ShapeDtypeStruct((rows, seq * wide) if flat else (chips, 2, rows, wide), BF16),
        in_specs=[vmem()] * len(pieces),
        out_specs=vmem(),
        compiler_params=PARAMS,
    )(*pieces)
    return joined if flat else joined.transpose(2, 0, 1, 3).reshape(rows, seq * wide)


def solution(mesh):
    placed = (
        P("seq", "head"),
        P("seq", "head"),
        P("seq", "head"),
        P("head"),
        P("seq", None),
        P("seq", "head"),
    )
    return jax.shard_map(
        local, mesh=mesh, in_specs=placed, out_specs=P(("seq", "head"), None), check_vma=False
    )
```

```python
import functools
import math

import jax
import jax.numpy as jnp
from jax import lax
from jax.experimental import pallas as pl
from jax.experimental.pallas import tpu as pltpu
from jax.sharding import PartitionSpec as P

BLOCK = 128
HALO = 64
NEGATIVE_FILL = -1e30
LAST = (((1,), (1,)), ((), ()))
BF16 = jnp.bfloat16
PARAMS = pltpu.CompilerParams(vmem_limit_bytes=32 << 20)


def vmem():
    return pl.BlockSpec(memory_space=pltpu.VMEM)


def smem():
    return pl.BlockSpec(memory_space=pltpu.SMEM)


def hbm():
    return pl.BlockSpec(memory_space=pltpu.HBM)


def shaped(*shape):
    return pltpu.VMEM(shape, BF16)


def far_away(*arrays):
    return [pltpu.with_memory_space_constraint(array, pltpu.HBM) for array in arrays]


def column_of(count, width, number):
    row = lax.broadcasted_iota(jnp.int32, (count, width), 0)
    found = jnp.zeros((count, width), jnp.int32)
    for r in range(count):
        found = jnp.where(row == r, number(r), found)
    return found


def pick_kernel(
    picks_ref, band_ref, q_hbm, k_hbm, v_hbm, summary_ref, halo_ref, width_ref, q_ref, k_ref, v_ref, sems
):
    per_block = picks_ref.shape[1]
    copies = [
        pltpu.make_async_copy(ref, into, sems.at[part])
        for part, (ref, into) in enumerate(((k_hbm, k_ref), (v_hbm, v_ref), (q_hbm, q_ref)))
    ]
    for copy in copies:
        copy.start()
    wanted = column_of(per_block, BLOCK, lambda r: picks_ref[0, r])
    width_ref[...] = column_of(*width_ref.shape, lambda r: band_ref[r])
    column = lax.broadcasted_iota(jnp.int32, (per_block, BLOCK), 1)
    chosen = jnp.where(column == wanted, 1.0, 0.0).astype(BF16)
    for part, ref in enumerate((k_ref, v_ref)):
        copies[part].wait()
        taken = jnp.dot(chosen, ref[...], preferred_element_type=jnp.float32)
        summary_ref[part] = taken.astype(BF16)
        halo_ref[part] = ref[BLOCK - HALO :, :]
    copies[2].wait()


def stack_kernel(*refs):
    for k, ref in enumerate(refs[:-1]):
        refs[-1][k] = ref[...]


def attend_kernel(width_ref, q_ref, k_ref, v_ref, halo_ref, mine_ref, other_ref, out_ref):
    size = BLOCK
    heads = q_ref.shape[1] // size
    chips, unused, per_block, unused = mine_ref.shape
    far_rows = chips * per_block
    place = lax.axis_index("seq")
    chip = place // 2
    core = lax.rem(place, 2)
    scale = 1.0 / math.sqrt(size)
    never = 4 * BLOCK
    own_gap = lax.broadcasted_iota(jnp.int32, (BLOCK, BLOCK), 0) - lax.broadcasted_iota(
        jnp.int32, (BLOCK, BLOCK), 1
    )
    own_gap = jnp.where(own_gap >= 0, own_gap, never)
    back_gap = lax.broadcasted_iota(jnp.int32, (BLOCK, HALO), 0) - lax.broadcasted_iota(
        jnp.int32, (BLOCK, HALO), 1
    )
    back_gap = jnp.where(place > 0, back_gap + HALO, never)
    far_chip = (lax.broadcasted_iota(jnp.int32, (BLOCK, far_rows), 1) // per_block) ^ chip
    mine_gap = jnp.where(far_chip * 2 + core < place, 0, never)
    other_gap = jnp.where(far_chip * 2 + (1 - core) < place, 0, never)
    gap = jnp.concatenate([own_gap, mine_gap, other_gap, back_gap], 1)
    for h in range(heads):
        cols = slice(h * size, (h + 1) * size)
        query = q_ref[:, cols]
        joined = [
            jnp.concatenate(
                [
                    own[:, cols],
                    mine_ref[:, part, :, cols].reshape(far_rows, size),
                    other_ref[:, part, :, cols].reshape(far_rows, size),
                    halo_ref[part, :, cols],
                ],
                0,
            )
            for part, own in enumerate((k_ref, v_ref))
        ]
        scores = lax.dot_general(query, joined[0], LAST, preferred_element_type=jnp.float32) * scale
        valid = gap < width_ref[h : h + 1, :]
        scores = jnp.where(valid, scores, NEGATIVE_FILL)
        largest = jnp.max(scores, axis=1, keepdims=True)
        weights = jnp.where(valid, jnp.exp(scores - largest), 0.0)
        total = jnp.sum(weights, axis=1, keepdims=True)
        mixed = jnp.dot(weights.astype(BF16), joined[1], preferred_element_type=jnp.float32)
        out_ref[:, cols] = (mixed / total).astype(BF16)


def cut_kernel(first_ref, second_ref, low_ref, high_ref):
    half = low_ref.shape[0]
    low_ref[...] = first_ref[:half]
    high_ref[...] = second_ref[half:]


def project_kernel(count, *refs):
    pieces, (mine_ref, other_ref) = refs[:count], refs[count : count + 2]
    send_ref, keep_ref = refs[-2:]
    core = lax.rem(lax.axis_index("seq"), 2)
    side = lax.rem(lax.axis_index("head"), 2)
    rows_in = []
    for parity in (1 - side, side):
        for ref in pieces:
            for j in range(ref.shape[0] // 2):
                rows_in.append(ref[2 * j + parity])
    rows_in = jnp.concatenate(rows_in, 0)
    for which, ref in ((core, mine_ref), (1 - core, other_ref)):
        found = lax.dot_general(rows_in, ref[...], LAST, preferred_element_type=jnp.float32)
        found = found.astype(BF16).reshape((2,) + send_ref.shape[1:])
        send_ref[which] = found[0]
        keep_ref[which] = found[1]


def split_kernel(came_ref, keep_ref, away_ref, stay_ref):
    side = lax.axis_index("head") // 2
    for ref, which in ((away_ref, 1 - side), (stay_ref, side)):
        total = came_ref[:, :, which].astype(jnp.float32) + keep_ref[:, :, which].astype(jnp.float32)
        ref[...] = total.astype(BF16)


def add_kernel(came_ref, stay_ref, *refs):
    for k, ref in enumerate(refs):
        ref[...] = (came_ref[:, k].astype(jnp.float32) + stay_ref[:, k].astype(jnp.float32)).astype(BF16)


def join_kernel(counts, *refs):
    out_ref = refs[-1]
    wide = refs[0].shape[-1]
    chip = lax.axis_index("seq") // 2
    at = 0
    for k, count in enumerate(counts):
        total = refs[at][...].reshape(2, -1, wide)
        if count == 2:
            more = refs[at + 1][...].reshape(2, -1, wide)
            total = (total.astype(jnp.float32) + more.astype(jnp.float32)).astype(BF16)
        at += count
        if len(out_ref.shape) == 4:
            out_ref[chip ^ k] = total
            continue
        for c in range(2):
            start = pl.multiple_of((chip ^ k) * (2 * wide), 128)
            out_ref[:, pl.ds(start + c * wide, wide)] = total[c]


def local(queries, keys, values, band, picks, w_out):
    heads = band.shape[0]
    tok_rows, feat = queries.shape
    per_block = picks.shape[1]
    seq = lax.axis_size("seq")
    groups = lax.axis_size("head")
    wide = w_out.shape[0]
    rows = tok_rows // groups
    chips = seq // 2
    half = groups // 2

    def swap(value, k, z):
        if k == 0:
            return lax.ppermute(value, "head", [(i, i ^ z) for i in range(groups)])
        if z == 0:
            return lax.ppermute(value, "seq", [(i, i ^ k) for i in range(seq)])
        pairs = [
            (s * groups + h, (s ^ k) * groups + (h ^ z)) for s in range(seq) for h in range(groups)
        ]
        return lax.ppermute(value, ("seq", "head"), pairs)

    other_w = swap(w_out, 1, 0)
    listed = BLOCK + HALO + seq * per_block
    summary, halo, width, queries, keys, values = pl.pallas_call(
        pick_kernel,
        out_shape=(
            shaped(2, per_block, feat),
            shaped(2, HALO, feat),
            pltpu.VMEM((heads, listed), jnp.int32),
        )
        + (shaped(tok_rows, feat),) * 3,
        in_specs=[smem(), smem(), hbm(), hbm(), hbm()],
        out_specs=(vmem(),) * 6,
        scratch_shapes=[pltpu.SemaphoreType.DMA((3,))],
        compiler_params=PARAMS,
    )(*far_away(picks, band, queries, keys, values))
    far = [summary] + [swap(summary, 2 * k, 0) for k in range(1, chips)]
    halo = lax.ppermute(halo, "seq", [(i, i + 1) for i in range(seq - 1)])
    mine = pl.pallas_call(
        stack_kernel,
        out_shape=shaped(chips, 2, per_block, feat),
        in_specs=[vmem()] * chips,
        out_specs=vmem(),
        compiler_params=PARAMS,
    )(*far)
    other = swap(mine, 1, 0)
    attention = pl.pallas_call(
        attend_kernel,
        out_shape=shaped(tok_rows, feat),
        in_specs=[vmem()] * 7,
        out_specs=vmem(),
        compiler_params=PARAMS,
    )(width, queries, keys, values, halo, mine, other)
    attention = attention.reshape(groups, rows, feat)
    parts = {k: [swap(attention, 2 * k, 0)] for k in range(1, chips) if k != 3}
    parts[0] = [attention]
    if chips > 3:
        low, high = pl.pallas_call(
            cut_kernel,
            out_shape=(shaped(half, rows, feat),) * 2,
            in_specs=[vmem()] * 2,
            out_specs=(vmem(),) * 2,
            compiler_params=PARAMS,
        )(parts[1][0], parts[2][0])
        parts[3] = [swap(low, 4, 0), swap(high, 2, 0)]
    order = [[0], [1, 2], [3]] + [[k] for k in range(4, chips)]
    found = {}
    after = {1: [low] if chips > 3 else [], 3: []}
    for group in order:
        group = [k for k in group if k < chips]
        if not group:
            continue
        n = len(group)
        pieces = [piece for k in group for piece in parts[k]]
        before = after.get(group[0], [])
        send, keep = pl.pallas_call(
            functools.partial(project_kernel, len(pieces)),
            out_shape=(shaped(2, n, half, rows, wide),) * 2,
            in_specs=[vmem()] * (len(pieces) + 2)
            + [pl.BlockSpec(memory_space=pl.ANY)] * len(before),
            out_specs=(vmem(), vmem()),
            compiler_params=PARAMS,
            cost_estimate=pl.CostEstimate(
                flops=40 * n * tok_rows * wide * feat, bytes_accessed=40 * wide * feat, transcendentals=0
            ),
        )(*pieces, w_out, other_w, *before)
        came = swap(send, 0, 1)
        away, stay = pl.pallas_call(
            split_kernel,
            out_shape=(shaped(2, n, rows, wide),) * 2,
            in_specs=[vmem()] * 2,
            out_specs=(vmem(), vmem()),
            compiler_params=PARAMS,
        )(came, keep)
        if n == 1 and group != [0]:
            k = group[0]
            found[k] = [swap(away, 2 * k, 2), swap(stay, 2 * k, 0)]
            continue
        sums = pl.pallas_call(
            add_kernel,
            out_shape=(shaped(2, rows, wide),) * n,
            in_specs=[vmem()] * 2,
            out_specs=(vmem(),) * n,
            compiler_params=PARAMS,
        )(swap(away, 0, 2), stay)
        if group == [0]:
            after[1].append(stay)
            after[3].append(sums[0])
        for k, value in zip(group, sums):
            found[k] = [swap(value, 2 * k, 0) if k else value]
    flat = wide % 128 == 0
    joined = pl.pallas_call(
        functools.partial(join_kernel, [len(found[k]) for k in range(chips)]),
        out_shape=jax.ShapeDtypeStruct((rows, seq * wide) if flat else (chips, 2, rows, wide), BF16),
        in_specs=[vmem()] * sum(len(value) for value in found.values()),
        out_specs=vmem(),
        compiler_params=PARAMS,
    )(*[piece for k in range(chips) for piece in found[k]])
    return joined if flat else joined.transpose(2, 0, 1, 3).reshape(rows, seq * wide)


def solution(mesh):
    placed = (
        P("seq", "head"),
        P("seq", "head"),
        P("seq", "head"),
        P("head"),
        P("seq", None),
        P("seq", "head"),
    )
    return jax.shard_map(
        local, mesh=mesh, in_specs=placed, out_specs=P(("seq", "head"), None), check_vma=False
    )
```

```python
import functools
import math

import jax
import jax.numpy as jnp
from jax import lax
from jax.experimental import pallas as pl
from jax.experimental.pallas import tpu as pltpu
from jax.sharding import PartitionSpec as P

BLOCK = 128
HALO = 64
NEGATIVE_FILL = -1e30
LAST = (((1,), (1,)), ((), ()))
BF16 = jnp.bfloat16
PARAMS = pltpu.CompilerParams(vmem_limit_bytes=32 << 20)


def vmem():
    return pl.BlockSpec(memory_space=pltpu.VMEM)


def smem():
    return pl.BlockSpec(memory_space=pltpu.SMEM)


def hbm():
    return pl.BlockSpec(memory_space=pltpu.HBM)


def shaped(*shape):
    return pltpu.VMEM(shape, BF16)


def far_away(*arrays):
    return [pltpu.with_memory_space_constraint(array, pltpu.HBM) for array in arrays]


def column_of(count, width, number):
    row = lax.broadcasted_iota(jnp.int32, (count, width), 0)
    found = jnp.zeros((count, width), jnp.int32)
    for r in range(count):
        found = jnp.where(row == r, number(r), found)
    return found


def bring_kernel(band_ref, q_hbm, k_hbm, v_hbm, halo_ref, width_ref, q_ref, k_ref, v_ref, sems):
    copies = [
        pltpu.make_async_copy(ref, into, sems.at[part])
        for part, (ref, into) in enumerate(((k_hbm, k_ref), (v_hbm, v_ref), (q_hbm, q_ref)))
    ]
    for copy in copies:
        copy.start()
    width_ref[...] = column_of(*width_ref.shape, lambda r: band_ref[r])
    for copy in copies:
        copy.wait()
    for part, ref in enumerate((k_ref, v_ref)):
        halo_ref[part] = ref[BLOCK - HALO :, :]


def pick_kernel(picks_ref, k_ref, v_ref, summary_ref):
    per_block = picks_ref.shape[1]
    wanted = column_of(per_block, BLOCK, lambda r: picks_ref[0, r])
    column = lax.broadcasted_iota(jnp.int32, (per_block, BLOCK), 1)
    chosen = jnp.where(column == wanted, 1.0, 0.0).astype(BF16)
    for part, ref in enumerate((k_ref, v_ref)):
        taken = jnp.dot(chosen, ref[...], preferred_element_type=jnp.float32)
        summary_ref[part] = taken.astype(BF16)


def stack_kernel(halo_ref, own_ref, *refs):
    for k, ref in enumerate(refs[:-1]):
        refs[-1][k] = ref[...]


def attend_own_kernel(width_ref, q_ref, k_ref, v_ref, top_ref, total_ref, sum_ref):
    size = BLOCK
    scale = 1.0 / math.sqrt(size)
    gap = lax.broadcasted_iota(jnp.int32, (BLOCK, BLOCK), 0) - lax.broadcasted_iota(
        jnp.int32, (BLOCK, BLOCK), 1
    )
    gap = jnp.where(gap >= 0, gap, 4 * BLOCK)
    for h in range(q_ref.shape[1] // size):
        cols = slice(h * size, (h + 1) * size)
        scores = lax.dot_general(q_ref[:, cols], k_ref[:, cols], LAST, preferred_element_type=jnp.float32)
        valid = gap < width_ref[h : h + 1, :BLOCK]
        scores = jnp.where(valid, scores * scale, NEGATIVE_FILL)
        largest = jnp.max(scores, axis=1, keepdims=True)
        weights = jnp.where(valid, jnp.exp(scores - largest), 0.0)
        top_ref[:, cols] = jnp.broadcast_to(largest, (BLOCK, size))
        total_ref[:, cols] = jnp.broadcast_to(jnp.sum(weights, axis=1, keepdims=True), (BLOCK, size))
        sum_ref[:, cols] = jnp.dot(weights.astype(BF16), v_ref[:, cols], preferred_element_type=jnp.float32)


def attend_kernel(
    width_ref, q_ref, top_ref, total_ref, sum_ref, halo_ref, mine_ref, other_ref, out_ref
):
    size = BLOCK
    heads = q_ref.shape[1] // size
    chips, unused, per_block, unused = mine_ref.shape
    far_rows = chips * per_block
    place = lax.axis_index("seq")
    chip = place // 2
    core = lax.rem(place, 2)
    scale = 1.0 / math.sqrt(size)
    never = 4 * BLOCK
    back_gap = lax.broadcasted_iota(jnp.int32, (BLOCK, HALO), 0) - lax.broadcasted_iota(
        jnp.int32, (BLOCK, HALO), 1
    )
    back_gap = jnp.where(place > 0, back_gap + HALO, never)
    far_chip = (lax.broadcasted_iota(jnp.int32, (BLOCK, far_rows), 1) // per_block) ^ chip
    mine_gap = jnp.where(far_chip * 2 + core < place, 0, never)
    other_gap = jnp.where(far_chip * 2 + (1 - core) < place, 0, never)
    gap = jnp.concatenate([mine_gap, other_gap, back_gap], 1)
    listed = gap.shape[1]
    for h in range(heads):
        cols = slice(h * size, (h + 1) * size)
        joined = [
            jnp.concatenate(
                [
                    mine_ref[:, part, :, cols].reshape(far_rows, size),
                    other_ref[:, part, :, cols].reshape(far_rows, size),
                    halo_ref[part, :, cols],
                ],
                0,
            )
            for part in range(2)
        ]
        scores = lax.dot_general(q_ref[:, cols], joined[0], LAST, preferred_element_type=jnp.float32)
        valid = gap < width_ref[h : h + 1, :listed]
        scores = jnp.where(valid, scores * scale, NEGATIVE_FILL)
        before = top_ref[:, cols]
        largest = jnp.maximum(before[:, :1], jnp.max(scores, axis=1, keepdims=True))
        weights = jnp.where(valid, jnp.exp(scores - largest), 0.0)
        factor = jnp.exp(before - largest)
        total = total_ref[:, cols] * factor + jnp.sum(weights, axis=1, keepdims=True)
        mixed = jnp.dot(weights.astype(BF16), joined[1], preferred_element_type=jnp.float32)
        out_ref[:, cols] = ((sum_ref[:, cols] * factor + mixed) / total).astype(BF16)


def cut_kernel(first_ref, second_ref, *refs):
    low_ref, high_ref = refs[-2:]
    half = low_ref.shape[0]
    low_ref[...] = first_ref[:half]
    high_ref[...] = second_ref[half:]


def project_kernel(count, *refs):
    pieces, (mine_ref, other_ref) = refs[:count], refs[count : count + 2]
    send_ref, keep_ref = refs[-2:]
    core = lax.rem(lax.axis_index("seq"), 2)
    side = lax.rem(lax.axis_index("head"), 2)
    rows_in = []
    for parity in (1 - side, side):
        for ref in pieces:
            for j in range(ref.shape[0] // 2):
                rows_in.append(ref[2 * j + parity])
    rows_in = jnp.concatenate(rows_in, 0)
    for which, ref in ((core, mine_ref), (1 - core, other_ref)):
        found = lax.dot_general(rows_in, ref[...], LAST, preferred_element_type=jnp.float32)
        found = found.astype(BF16).reshape((2,) + send_ref.shape[1:])
        send_ref[which] = found[0]
        keep_ref[which] = found[1]


def split_kernel(came_ref, keep_ref, *refs):
    side = lax.axis_index("head") // 2
    for k in range(len(refs) // 2):
        for ref, which in ((refs[2 * k], 1 - side), (refs[2 * k + 1], side)):
            total = came_ref[:, k, which].astype(jnp.float32) + keep_ref[:, k, which].astype(jnp.float32)
            ref[...] = total.astype(BF16)


def join_kernel(*refs):
    out_ref = refs[-1]
    wide = refs[0].shape[-1]
    chip = lax.axis_index("seq") // 2
    for k in range(len(refs) // 2):
        total = refs[2 * k][...].astype(jnp.float32) + refs[2 * k + 1][...].astype(jnp.float32)
        total = total.astype(BF16)
        if len(out_ref.shape) == 4:
            out_ref[chip ^ k] = total
            continue
        for c in range(2):
            start = pl.multiple_of((chip ^ k) * (2 * wide), 128)
            out_ref[:, pl.ds(start + c * wide, wide)] = total[c]


def local(queries, keys, values, band, picks, w_out):
    heads = band.shape[0]
    tok_rows, feat = queries.shape
    per_block = picks.shape[1]
    seq = lax.axis_size("seq")
    groups = lax.axis_size("head")
    wide = w_out.shape[0]
    rows = tok_rows // groups
    chips = seq // 2
    half = groups // 2

    def swap(value, k, z):
        if k == 0:
            return lax.ppermute(value, "head", [(i, i ^ z) for i in range(groups)])
        if z == 0:
            return lax.ppermute(value, "seq", [(i, i ^ k) for i in range(seq)])
        pairs = [
            (s * groups + h, (s ^ k) * groups + (h ^ z)) for s in range(seq) for h in range(groups)
        ]
        return lax.ppermute(value, ("seq", "head"), pairs)

    other_w = swap(w_out, 1, 0)
    listed = max(BLOCK, HALO + seq * per_block)
    halo, width, queries, keys, values = pl.pallas_call(
        bring_kernel,
        out_shape=(shaped(2, HALO, feat), pltpu.VMEM((heads, listed), jnp.int32))
        + (shaped(tok_rows, feat),) * 3,
        in_specs=[smem(), hbm(), hbm(), hbm()],
        out_specs=(vmem(),) * 5,
        scratch_shapes=[pltpu.SemaphoreType.DMA((3,))],
        compiler_params=PARAMS,
    )(*far_away(band, queries, keys, values))
    halo = lax.ppermute(halo, "seq", [(i, i + 1) for i in range(seq - 1)])
    summary = pl.pallas_call(
        pick_kernel,
        out_shape=shaped(2, per_block, feat),
        in_specs=[smem(), vmem(), vmem()],
        out_specs=vmem(),
        compiler_params=PARAMS,
    )(*far_away(picks), keys, values)
    far = [summary] + [swap(summary, 2 * k, 0) for k in range(1, chips)]
    own = pl.pallas_call(
        attend_own_kernel,
        out_shape=(pltpu.VMEM((tok_rows, feat), jnp.float32),) * 3,
        in_specs=[vmem()] * 4,
        out_specs=(vmem(),) * 3,
        compiler_params=PARAMS,
    )(width, queries, keys, values)
    mine = pl.pallas_call(
        stack_kernel,
        out_shape=shaped(chips, 2, per_block, feat),
        in_specs=[pl.BlockSpec(memory_space=pl.ANY)] * 2 + [vmem()] * chips,
        out_specs=vmem(),
        compiler_params=PARAMS,
    )(halo, own[0], *far)
    other = swap(mine, 1, 0)
    attention = pl.pallas_call(
        attend_kernel,
        out_shape=shaped(tok_rows, feat),
        in_specs=[vmem()] * 8,
        out_specs=vmem(),
        compiler_params=PARAMS,
    )(width, queries, *own, halo, mine, other)
    attention = attention.reshape(groups, rows, feat)
    parts = {k: [swap(attention, 2 * k, 0)] for k in range(1, chips) if k != 3}
    parts[0] = [attention]
    order = [[0], [1, 2], [3]] + [[k] for k in range(4, chips)]
    found = {}
    before = []
    for group in order:
        group = [k for k in group if k < chips]
        if not group:
            continue
        n = len(group)
        if group == [3]:
            low, high = pl.pallas_call(
                cut_kernel,
                out_shape=(shaped(half, rows, feat),) * 2,
                in_specs=[vmem()] * 2 + [pl.BlockSpec(memory_space=pl.ANY)] * 2,
                out_specs=(vmem(),) * 2,
                compiler_params=PARAMS,
            )(parts[1][0], parts[2][0], before[0], found[0][1])
            parts[3] = [swap(low, 4, 0), swap(high, 2, 0)]
            before = [found[0][0]]
        pieces = [piece for k in group for piece in parts[k]]
        send, keep = pl.pallas_call(
            functools.partial(project_kernel, len(pieces)),
            out_shape=(shaped(2, n, half, rows, wide),) * 2,
            in_specs=[vmem()] * (len(pieces) + 2)
            + [pl.BlockSpec(memory_space=pl.ANY)] * len(before),
            out_specs=(vmem(), vmem()),
            compiler_params=PARAMS,
        )(*pieces, w_out, other_w, *before)
        before = [keep]
        came = swap(send, 0, 1)
        parted = pl.pallas_call(
            split_kernel,
            out_shape=(shaped(2, rows, wide),) * (2 * n),
            in_specs=[vmem()] * 2,
            out_specs=(vmem(),) * (2 * n),
            compiler_params=PARAMS,
        )(came, keep)
        for k, away, stay in zip(group, parted[::2], parted[1::2]):
            found[k] = [swap(away, 2 * k, 2), swap(stay, 2 * k, 0) if k else stay]
    flat = wide % 128 == 0
    joined = pl.pallas_call(
        join_kernel,
        out_shape=jax.ShapeDtypeStruct((rows, seq * wide) if flat else (chips, 2, rows, wide), BF16),
        in_specs=[vmem()] * (2 * chips),
        out_specs=vmem(),
        compiler_params=PARAMS,
    )(*[piece for k in range(chips) for piece in found[k]])
    return joined if flat else joined.transpose(2, 0, 1, 3).reshape(rows, seq * wide)


def solution(mesh):
    placed = (
        P("seq", "head"),
        P("seq", "head"),
        P("seq", "head"),
        P("head"),
        P("seq", None),
        P("seq", "head"),
    )
    return jax.shard_map(
        local, mesh=mesh, in_specs=placed, out_specs=P(("seq", "head"), None), check_vma=False
    )
```

```python
import functools
import math

import jax
import jax.numpy as jnp
from jax import lax
from jax.experimental import pallas as pl
from jax.experimental.pallas import tpu as pltpu
from jax.sharding import PartitionSpec as P

BLOCK = 128
HALO = 64
NEGATIVE_FILL = -1e30
LAST = (((1,), (1,)), ((), ()))
BF16 = jnp.bfloat16
PARAMS = pltpu.CompilerParams(vmem_limit_bytes=32 << 20)


def vmem():
    return pl.BlockSpec(memory_space=pltpu.VMEM)


def smem():
    return pl.BlockSpec(memory_space=pltpu.SMEM)


def hbm():
    return pl.BlockSpec(memory_space=pltpu.HBM)


def shaped(*shape):
    return pltpu.VMEM(shape, BF16)


def far_away(*arrays):
    return [pltpu.with_memory_space_constraint(array, pltpu.HBM) for array in arrays]


def column_of(count, width, number):
    row = lax.broadcasted_iota(jnp.int32, (count, width), 0)
    found = jnp.zeros((count, width), jnp.int32)
    for r in range(count):
        found = jnp.where(row == r, number(r), found)
    return found


def pick_kernel(
    picks_ref, band_ref, q_hbm, k_hbm, v_hbm, summary_ref, halo_ref, width_ref, q_ref, k_ref, v_ref, sems
):
    per_block = picks_ref.shape[1]
    copies = [
        pltpu.make_async_copy(ref, into, sems.at[part])
        for part, (ref, into) in enumerate(((k_hbm, k_ref), (v_hbm, v_ref), (q_hbm, q_ref)))
    ]
    for copy in copies:
        copy.start()
    wanted = column_of(per_block, BLOCK, lambda r: picks_ref[0, r])
    width_ref[...] = column_of(*width_ref.shape, lambda r: band_ref[r])
    column = lax.broadcasted_iota(jnp.int32, (per_block, BLOCK), 1)
    chosen = jnp.where(column == wanted, 1.0, 0.0).astype(BF16)
    for part, ref in enumerate((k_ref, v_ref)):
        copies[part].wait()
        taken = jnp.dot(chosen, ref[...], preferred_element_type=jnp.float32)
        summary_ref[part] = taken.astype(BF16)
        halo_ref[part] = ref[BLOCK - HALO :, :]
    copies[2].wait()


def stack_kernel(*refs):
    for k, ref in enumerate(refs[:-1]):
        refs[-1][k] = ref[...]


def attend_kernel(width_ref, q_ref, k_ref, v_ref, halo_ref, mine_ref, other_ref, out_ref):
    size = BLOCK
    heads = q_ref.shape[1] // size
    chips, unused, per_block, unused = mine_ref.shape
    far_rows = chips * per_block
    place = lax.axis_index("seq")
    chip = place // 2
    core = lax.rem(place, 2)
    scale = 1.0 / math.sqrt(size)
    never = 4 * BLOCK
    own_gap = lax.broadcasted_iota(jnp.int32, (BLOCK, BLOCK), 0) - lax.broadcasted_iota(
        jnp.int32, (BLOCK, BLOCK), 1
    )
    own_gap = jnp.where(own_gap >= 0, own_gap, never)
    back_gap = lax.broadcasted_iota(jnp.int32, (BLOCK, HALO), 0) - lax.broadcasted_iota(
        jnp.int32, (BLOCK, HALO), 1
    )
    back_gap = jnp.where(place > 0, back_gap + HALO, never)
    far_chip = (lax.broadcasted_iota(jnp.int32, (BLOCK, far_rows), 1) // per_block) ^ chip
    mine_gap = jnp.where(far_chip * 2 + core < place, 0, never)
    other_gap = jnp.where(far_chip * 2 + (1 - core) < place, 0, never)
    gap = jnp.concatenate([own_gap, mine_gap, other_gap, back_gap], 1)
    for h in range(heads):
        cols = slice(h * size, (h + 1) * size)
        query = q_ref[:, cols]
        joined = [
            jnp.concatenate(
                [
                    own[:, cols],
                    mine_ref[:, part, :, cols].reshape(far_rows, size),
                    other_ref[:, part, :, cols].reshape(far_rows, size),
                    halo_ref[part, :, cols],
                ],
                0,
            )
            for part, own in enumerate((k_ref, v_ref))
        ]
        scores = lax.dot_general(query, joined[0], LAST, preferred_element_type=jnp.float32) * scale
        valid = gap < width_ref[h : h + 1, :]
        scores = jnp.where(valid, scores, NEGATIVE_FILL)
        largest = jnp.max(scores, axis=1, keepdims=True)
        weights = jnp.where(valid, jnp.exp(scores - largest), 0.0)
        total = jnp.sum(weights, axis=1, keepdims=True)
        mixed = jnp.dot(weights.astype(BF16), joined[1], preferred_element_type=jnp.float32)
        out_ref[:, cols] = (mixed / total).astype(BF16)


def cut_kernel(first_ref, second_ref, *refs):
    low_ref, high_ref = refs[-2:]
    half = low_ref.shape[0]
    low_ref[...] = first_ref[:half]
    high_ref[...] = second_ref[half:]


def project_kernel(count, chunks, *refs):
    pieces, (mine_ref, other_ref) = refs[:count], refs[count : count + 2]
    send_refs, keep_refs = refs[-2 * chunks : -chunks], refs[-chunks:]
    core = lax.rem(lax.axis_index("seq"), 2)
    side = lax.rem(lax.axis_index("head"), 2)
    rows_in = []
    for parity in (1 - side, side):
        for ref in pieces:
            for j in range(ref.shape[0] // 2):
                rows_in.append(ref[2 * j + parity])
    rows_in = jnp.concatenate(rows_in, 0)
    for which, ref in ((core, mine_ref), (1 - core, other_ref)):
        found = lax.dot_general(rows_in, ref[...], LAST, preferred_element_type=jnp.float32)
        found = found.astype(BF16).reshape((2, chunks) + send_refs[0].shape[1:])
        for k in range(chunks):
            send_refs[k][which] = found[0, k]
            keep_refs[k][which] = found[1, k]


def split_kernel(late, came_ref, keep_ref, *refs):
    away_ref, stay_ref = refs[-2 - late : len(refs) - late]
    side = lax.axis_index("head") // 2
    for ref, which in ((away_ref, 1 - side), (stay_ref, side)):
        total = came_ref[:, which].astype(jnp.float32) + keep_ref[:, which].astype(jnp.float32)
        ref[...] = total.astype(BF16)
    if late:
        refs[-1][...] = refs[0][...]


def join_kernel(*refs):
    out_ref = refs[-1]
    wide = refs[0].shape[-1]
    chip = lax.axis_index("seq") // 2
    for k in range(len(refs) // 2):
        total = refs[2 * k][...].astype(jnp.float32) + refs[2 * k + 1][...].astype(jnp.float32)
        total = total.astype(BF16)
        if len(out_ref.shape) == 4:
            out_ref[chip ^ k] = total
            continue
        for c in range(2):
            start = pl.multiple_of((chip ^ k) * (2 * wide), 128)
            out_ref[:, pl.ds(start + c * wide, wide)] = total[c]


def local(queries, keys, values, band, picks, w_out):
    heads = band.shape[0]
    tok_rows, feat = queries.shape
    per_block = picks.shape[1]
    seq = lax.axis_size("seq")
    groups = lax.axis_size("head")
    wide = w_out.shape[0]
    rows = tok_rows // groups
    chips = seq // 2
    half = groups // 2

    def swap(value, k, z):
        if k == 0:
            return lax.ppermute(value, "head", [(i, i ^ z) for i in range(groups)])
        if z == 0:
            return lax.ppermute(value, "seq", [(i, i ^ k) for i in range(seq)])
        pairs = [
            (s * groups + h, (s ^ k) * groups + (h ^ z)) for s in range(seq) for h in range(groups)
        ]
        return lax.ppermute(value, ("seq", "head"), pairs)

    other_w = swap(w_out, 1, 0)
    listed = BLOCK + HALO + seq * per_block
    summary, halo, width, queries, keys, values = pl.pallas_call(
        pick_kernel,
        out_shape=(
            shaped(2, per_block, feat),
            shaped(2, HALO, feat),
            pltpu.VMEM((heads, listed), jnp.int32),
        )
        + (shaped(tok_rows, feat),) * 3,
        in_specs=[smem(), smem(), hbm(), hbm(), hbm()],
        out_specs=(vmem(),) * 6,
        scratch_shapes=[pltpu.SemaphoreType.DMA((3,))],
        compiler_params=PARAMS,
    )(*far_away(picks, band, queries, keys, values))
    far = [summary] + [swap(summary, 2 * k, 0) for k in range(1, chips)]
    halo = lax.ppermute(halo, "seq", [(i, i + 1) for i in range(seq - 1)])
    mine = pl.pallas_call(
        stack_kernel,
        out_shape=shaped(chips, 2, per_block, feat),
        in_specs=[vmem()] * chips,
        out_specs=vmem(),
        compiler_params=PARAMS,
    )(*far)
    other = swap(mine, 1, 0)
    attention = pl.pallas_call(
        attend_kernel,
        out_shape=shaped(tok_rows, feat),
        in_specs=[vmem()] * 7,
        out_specs=vmem(),
        compiler_params=PARAMS,
    )(width, queries, keys, values, halo, mine, other)
    attention = attention.reshape(groups, rows, feat)
    parts = {k: [swap(attention, 2 * k, 0)] for k in range(1, chips) if k != 3}
    parts[0] = [attention]
    found, stays = {}, {}

    def after(*arrays):
        return [pl.BlockSpec(memory_space=pl.ANY)] * len(arrays), arrays

    def projected(group, order):
        pieces = [piece for k in group for piece in parts[k]]
        n = len(group)
        specs, arrays = after(*order)
        return pl.pallas_call(
            functools.partial(project_kernel, len(pieces), n),
            out_shape=(shaped(2, half, rows, wide),) * (2 * n),
            in_specs=[vmem()] * (len(pieces) + 2) + specs,
            out_specs=(vmem(),) * (2 * n),
            compiler_params=PARAMS,
            cost_estimate=pl.CostEstimate(
                flops=4 * n * tok_rows * wide * feat, bytes_accessed=4 * wide * feat, transcendentals=0
            ),
        )(*pieces, w_out, other_w, *arrays)

    def exchanged(k, send, keep, order=()):
        came = swap(send, 0, 1)
        late = k > 1
        specs, arrays = after(*order)
        parted = pl.pallas_call(
            functools.partial(split_kernel, late),
            out_shape=(shaped(2, rows, wide),) * (2 + late),
            in_specs=[vmem()] * (2 + late) + specs,
            out_specs=(vmem(),) * (2 + late),
            compiler_params=PARAMS,
        )(came, keep, *([stays[k - 1]] if late else []), *arrays)
        stays[k] = parted[1]
        found[k] = [swap(parted[0], 2 * k, 2), stays[k]]
        if late:
            found[k - 1][1] = swap(parted[2], 2 * (k - 1), 0)

    exchanged(0, *projected([0], ()))
    pair = [k for k in (1, 2) if k < chips]
    if pair:
        results = projected(pair, (stays[0],))
        for k, send, keep in zip(pair, results, results[len(pair) :]):
            exchanged(k, send, keep, found[1][:1] if k == 2 else ())
    if chips > 3:
        specs, arrays = after(*(results[-1], found[0][0]))
        low, high = pl.pallas_call(
            cut_kernel,
            out_shape=(shaped(half, rows, feat),) * 2,
            in_specs=[vmem()] * 2 + specs,
            out_specs=(vmem(),) * 2,
            compiler_params=PARAMS,
        )(parts[1][0], parts[2][0], *arrays)
        parts[3] = [swap(low, 4, 0), swap(high, 2, 0)]
    for k in range(3, chips):
        exchanged(k, *projected([k], (stays[1],)), (found[1][1:]) if k == 3 else ())
    if chips > 1:
        found[chips - 1][1] = swap(stays[chips - 1], 2 * (chips - 1), 0)
    flat = wide % 128 == 0
    joined = pl.pallas_call(
        join_kernel,
        out_shape=jax.ShapeDtypeStruct((rows, seq * wide) if flat else (chips, 2, rows, wide), BF16),
        in_specs=[vmem()] * (2 * chips),
        out_specs=vmem(),
        compiler_params=PARAMS,
    )(*[piece for k in range(chips) for piece in found[k]])
    return joined if flat else joined.transpose(2, 0, 1, 3).reshape(rows, seq * wide)


def solution(mesh):
    placed = (
        P("seq", "head"),
        P("seq", "head"),
        P("seq", "head"),
        P("head"),
        P("seq", None),
        P("seq", "head"),
    )
    return jax.shard_map(
        local, mesh=mesh, in_specs=placed, out_specs=P(("seq", "head"), None), check_vma=False
    )
```

```python
import functools
import math

import jax
import jax.numpy as jnp
from jax import lax
from jax.experimental import pallas as pl
from jax.experimental.pallas import tpu as pltpu
from jax.sharding import PartitionSpec as P

BLOCK = 128
HALO = 64
NEGATIVE_FILL = -1e30
LAST = (((1,), (1,)), ((), ()))
BF16 = jnp.bfloat16
PARAMS = pltpu.CompilerParams(vmem_limit_bytes=32 << 20)


def vmem():
    return pl.BlockSpec(memory_space=pltpu.VMEM)


def smem():
    return pl.BlockSpec(memory_space=pltpu.SMEM)


def hbm():
    return pl.BlockSpec(memory_space=pltpu.HBM)


def shaped(*shape):
    return pltpu.VMEM(shape, BF16)


def far_away(*arrays):
    return [pltpu.with_memory_space_constraint(array, pltpu.HBM) for array in arrays]


def column_of(count, width, number):
    row = lax.broadcasted_iota(jnp.int32, (count, width), 0)
    found = jnp.zeros((count, width), jnp.int32)
    for r in range(count):
        found = jnp.where(row == r, number(r), found)
    return found


def pick_kernel(
    picks_ref, band_ref, q_hbm, k_hbm, v_hbm, summary_ref, halo_ref, width_ref, q_ref, k_ref, v_ref, sems
):
    per_block = picks_ref.shape[1]
    copies = [
        pltpu.make_async_copy(ref, into, sems.at[part])
        for part, (ref, into) in enumerate(((k_hbm, k_ref), (v_hbm, v_ref), (q_hbm, q_ref)))
    ]
    for copy in copies:
        copy.start()
    wanted = column_of(per_block, BLOCK, lambda r: picks_ref[0, r])
    width_ref[...] = column_of(*width_ref.shape, lambda r: band_ref[r])
    column = lax.broadcasted_iota(jnp.int32, (per_block, BLOCK), 1)
    chosen = jnp.where(column == wanted, 1.0, 0.0).astype(BF16)
    for part, ref in enumerate((k_ref, v_ref)):
        copies[part].wait()
        taken = jnp.dot(chosen, ref[...], preferred_element_type=jnp.float32)
        summary_ref[part] = taken.astype(BF16)
        halo_ref[part] = ref[BLOCK - HALO :, :]
    copies[2].wait()


def stack_kernel(*refs):
    for k, ref in enumerate(refs[:-1]):
        refs[-1][k] = ref[...]


def attend_kernel(width_ref, q_ref, k_ref, v_ref, halo_ref, mine_ref, other_ref, out_ref):
    size = BLOCK
    heads = q_ref.shape[1] // size
    chips, unused, per_block, unused = mine_ref.shape
    far_rows = chips * per_block
    place = lax.axis_index("seq")
    chip = place // 2
    core = lax.rem(place, 2)
    scale = 1.0 / math.sqrt(size)
    never = 4 * BLOCK
    own_gap = lax.broadcasted_iota(jnp.int32, (BLOCK, BLOCK), 0) - lax.broadcasted_iota(
        jnp.int32, (BLOCK, BLOCK), 1
    )
    own_gap = jnp.where(own_gap >= 0, own_gap, never)
    back_gap = lax.broadcasted_iota(jnp.int32, (BLOCK, HALO), 0) - lax.broadcasted_iota(
        jnp.int32, (BLOCK, HALO), 1
    )
    back_gap = jnp.where(place > 0, back_gap + HALO, never)
    far_chip = (lax.broadcasted_iota(jnp.int32, (BLOCK, far_rows), 1) // per_block) ^ chip
    mine_gap = jnp.where(far_chip * 2 + core < place, 0, never)
    other_gap = jnp.where(far_chip * 2 + (1 - core) < place, 0, never)
    gap = jnp.concatenate([own_gap, mine_gap, other_gap, back_gap], 1)
    for h in range(heads):
        cols = slice(h * size, (h + 1) * size)
        query = q_ref[:, cols]
        joined = [
            jnp.concatenate(
                [
                    own[:, cols],
                    mine_ref[:, part, :, cols].reshape(far_rows, size),
                    other_ref[:, part, :, cols].reshape(far_rows, size),
                    halo_ref[part, :, cols],
                ],
                0,
            )
            for part, own in enumerate((k_ref, v_ref))
        ]
        scores = lax.dot_general(query, joined[0], LAST, preferred_element_type=jnp.float32) * scale
        valid = gap < width_ref[h : h + 1, :]
        scores = jnp.where(valid, scores, NEGATIVE_FILL)
        largest = jnp.max(scores, axis=1, keepdims=True)
        weights = jnp.where(valid, jnp.exp(scores - largest), 0.0)
        total = jnp.sum(weights, axis=1, keepdims=True)
        mixed = jnp.dot(weights.astype(BF16), joined[1], preferred_element_type=jnp.float32)
        out_ref[:, cols] = (mixed / total).astype(BF16)


def cut_kernel(first_ref, second_ref, *refs):
    low_ref, high_ref = refs[-2:]
    half = low_ref.shape[0]
    low_ref[...] = first_ref[:half]
    high_ref[...] = second_ref[half:]


def project_kernel(count, chunks, *refs):
    pieces, (mine_ref, other_ref) = refs[:count], refs[count : count + 2]
    send_refs, keep_refs = refs[-2 * chunks : -chunks], refs[-chunks:]
    core = lax.rem(lax.axis_index("seq"), 2)
    side = lax.rem(lax.axis_index("head"), 2)
    rows_in = []
    for parity in (1 - side, side):
        for ref in pieces:
            for j in range(ref.shape[0] // 2):
                rows_in.append(ref[2 * j + parity])
    rows_in = jnp.concatenate(rows_in, 0)
    for which, ref in ((core, mine_ref), (1 - core, other_ref)):
        found = lax.dot_general(rows_in, ref[...], LAST, preferred_element_type=jnp.float32)
        found = found.astype(BF16).reshape((2, chunks) + send_refs[0].shape[1:])
        for k in range(chunks):
            send_refs[k][which] = found[0, k]
            keep_refs[k][which] = found[1, k]


def split_kernel(late, came_ref, keep_ref, *refs):
    away_ref, stay_ref = refs[-2 - late : len(refs) - late]
    side = lax.axis_index("head") // 2
    for ref, which in ((away_ref, 1 - side), (stay_ref, side)):
        total = came_ref[:, which].astype(jnp.float32) + keep_ref[:, which].astype(jnp.float32)
        ref[...] = total.astype(BF16)
    if late:
        refs[-1][...] = refs[0][...]


def join_kernel(*refs):
    out_ref = refs[-1]
    wide = refs[0].shape[-1]
    chip = lax.axis_index("seq") // 2
    for k in range(len(refs) // 2):
        total = refs[2 * k][...].astype(jnp.float32) + refs[2 * k + 1][...].astype(jnp.float32)
        total = total.astype(BF16)
        if len(out_ref.shape) == 4:
            out_ref[chip ^ k] = total
            continue
        for c in range(2):
            start = pl.multiple_of((chip ^ k) * (2 * wide), 128)
            out_ref[:, pl.ds(start + c * wide, wide)] = total[c]


def local(queries, keys, values, band, picks, w_out):
    heads = band.shape[0]
    tok_rows, feat = queries.shape
    per_block = picks.shape[1]
    seq = lax.axis_size("seq")
    groups = lax.axis_size("head")
    wide = w_out.shape[0]
    rows = tok_rows // groups
    chips = seq // 2
    half = groups // 2

    def swap(value, k, z):
        if k == 0:
            return lax.ppermute(value, "head", [(i, i ^ z) for i in range(groups)])
        if z == 0:
            return lax.ppermute(value, "seq", [(i, i ^ k) for i in range(seq)])
        pairs = [
            (s * groups + h, (s ^ k) * groups + (h ^ z)) for s in range(seq) for h in range(groups)
        ]
        return lax.ppermute(value, ("seq", "head"), pairs)

    other_w = swap(w_out, 1, 0)
    listed = BLOCK + HALO + seq * per_block
    summary, halo, width, queries, keys, values = pl.pallas_call(
        pick_kernel,
        out_shape=(
            shaped(2, per_block, feat),
            shaped(2, HALO, feat),
            pltpu.VMEM((heads, listed), jnp.int32),
        )
        + (shaped(tok_rows, feat),) * 3,
        in_specs=[smem(), smem(), hbm(), hbm(), hbm()],
        out_specs=(vmem(),) * 6,
        scratch_shapes=[pltpu.SemaphoreType.DMA((3,))],
        compiler_params=PARAMS,
    )(*far_away(picks, band, queries, keys, values))
    far = [summary] + [swap(summary, 2 * k, 0) for k in range(1, chips)]
    halo = lax.ppermute(halo, "seq", [(i, i + 1) for i in range(seq - 1)])
    mine = pl.pallas_call(
        stack_kernel,
        out_shape=shaped(chips, 2, per_block, feat),
        in_specs=[vmem()] * chips,
        out_specs=vmem(),
        compiler_params=PARAMS,
    )(*far)
    other = swap(mine, 1, 0)
    attention = pl.pallas_call(
        attend_kernel,
        out_shape=shaped(tok_rows, feat),
        in_specs=[vmem()] * 7,
        out_specs=vmem(),
        compiler_params=PARAMS,
    )(width, queries, keys, values, halo, mine, other)
    attention = attention.reshape(groups, rows, feat)
    parts = {k: [swap(attention, 2 * k, 0)] for k in range(1, chips) if k != 3}
    parts[0] = [attention]
    found, stays = {}, {}

    def after(*arrays):
        return [pl.BlockSpec(memory_space=pl.ANY)] * len(arrays), arrays

    def projected(group, order):
        pieces = [piece for k in group for piece in parts[k]]
        n = len(group)
        specs, arrays = after(*order)
        return pl.pallas_call(
            functools.partial(project_kernel, len(pieces), n),
            out_shape=(shaped(2, half, rows, wide),) * (2 * n),
            in_specs=[vmem()] * (len(pieces) + 2) + specs,
            out_specs=(vmem(),) * (2 * n),
            compiler_params=PARAMS,
            cost_estimate=pl.CostEstimate(
                flops=4 * n * tok_rows * wide * feat, bytes_accessed=4 * wide * feat, transcendentals=0
            ),
        )(*pieces, w_out, other_w, *arrays)

    def exchanged(k, send, keep, order=()):
        came = swap(send, 0, 1)
        late = k > 1
        specs, arrays = after(*order)
        parted = pl.pallas_call(
            functools.partial(split_kernel, late),
            out_shape=(shaped(2, rows, wide),) * (2 + late),
            in_specs=[vmem()] * (2 + late) + specs,
            out_specs=(vmem(),) * (2 + late),
            compiler_params=PARAMS,
        )(came, keep, *([stays[k - 1]] if late else []), *arrays)
        stays[k] = parted[1]
        found[k] = [swap(parted[0], 2 * k, 2), stays[k]]
        if late:
            found[k - 1][1] = swap(parted[2], 2 * (k - 1), 0)

    exchanged(0, *projected([0], ()))
    pair = [k for k in (1, 2) if k < chips]
    if pair:
        results = projected(pair, (stays[0],))
        for k, send, keep in zip(pair, results, results[len(pair) :]):
            exchanged(k, send, keep, () if k == 2 else ())
    if chips > 3:
        specs, arrays = after(*(results[-1], found[0][0]))
        low, high = pl.pallas_call(
            cut_kernel,
            out_shape=(shaped(half, rows, feat),) * 2,
            in_specs=[vmem()] * 2 + specs,
            out_specs=(vmem(),) * 2,
            compiler_params=PARAMS,
        )(parts[1][0], parts[2][0], *arrays)
        parts[3] = [swap(low, 4, 0), swap(high, 2, 0)]
    for k in range(3, chips):
        exchanged(k, *projected([k], (stays[1],)))
    if chips > 1:
        found[chips - 1][1] = swap(stays[chips - 1], 2 * (chips - 1), 0)
    flat = wide % 128 == 0
    joined = pl.pallas_call(
        join_kernel,
        out_shape=jax.ShapeDtypeStruct((rows, seq * wide) if flat else (chips, 2, rows, wide), BF16),
        in_specs=[vmem()] * (2 * chips),
        out_specs=vmem(),
        compiler_params=PARAMS,
    )(*[piece for k in range(chips) for piece in found[k]])
    return joined if flat else joined.transpose(2, 0, 1, 3).reshape(rows, seq * wide)


def solution(mesh):
    placed = (
        P("seq", "head"),
        P("seq", "head"),
        P("seq", "head"),
        P("head"),
        P("seq", None),
        P("seq", "head"),
    )
    return jax.shard_map(
        local, mesh=mesh, in_specs=placed, out_specs=P(("seq", "head"), None), check_vma=False
    )
```

```python
import functools
import math

import jax
import jax.numpy as jnp
from jax import lax
from jax.experimental import pallas as pl
from jax.experimental.pallas import tpu as pltpu
from jax.sharding import PartitionSpec as P

BLOCK = 128
HALO = 64
NEGATIVE_FILL = -1e30
LAST = (((1,), (1,)), ((), ()))
BF16 = jnp.bfloat16
PARAMS = pltpu.CompilerParams(vmem_limit_bytes=32 << 20)


def vmem():
    return pl.BlockSpec(memory_space=pltpu.VMEM)


def smem():
    return pl.BlockSpec(memory_space=pltpu.SMEM)


def hbm():
    return pl.BlockSpec(memory_space=pltpu.HBM)


def shaped(*shape):
    return pltpu.VMEM(shape, BF16)


def far_away(*arrays):
    return [pltpu.with_memory_space_constraint(array, pltpu.HBM) for array in arrays]


def column_of(count, width, number):
    row = lax.broadcasted_iota(jnp.int32, (count, width), 0)
    found = jnp.zeros((count, width), jnp.int32)
    for r in range(count):
        found = jnp.where(row == r, number(r), found)
    return found


def pick_kernel(
    picks_ref, band_ref, q_hbm, k_hbm, v_hbm, summary_ref, halo_ref, width_ref, q_ref, k_ref, v_ref, sems
):
    per_block = picks_ref.shape[1]
    copies = [
        pltpu.make_async_copy(ref, into, sems.at[part])
        for part, (ref, into) in enumerate(((k_hbm, k_ref), (v_hbm, v_ref), (q_hbm, q_ref)))
    ]
    for copy in copies:
        copy.start()
    wanted = column_of(per_block, BLOCK, lambda r: picks_ref[0, r])
    width_ref[...] = column_of(*width_ref.shape, lambda r: band_ref[r])
    column = lax.broadcasted_iota(jnp.int32, (per_block, BLOCK), 1)
    chosen = jnp.where(column == wanted, 1.0, 0.0).astype(BF16)
    for part, ref in enumerate((k_ref, v_ref)):
        copies[part].wait()
        taken = jnp.dot(chosen, ref[...], preferred_element_type=jnp.float32)
        summary_ref[part] = taken.astype(BF16)
        halo_ref[part] = ref[BLOCK - HALO :, :]
    copies[2].wait()


def stack_kernel(*refs):
    for k, ref in enumerate(refs[:-1]):
        refs[-1][k] = ref[...]


def attend_kernel(width_ref, q_ref, k_ref, v_ref, halo_ref, mine_ref, other_ref, out_ref):
    size = BLOCK
    heads = q_ref.shape[1] // size
    chips, unused, per_block, unused = mine_ref.shape
    far_rows = chips * per_block
    place = lax.axis_index("seq")
    chip = place // 2
    core = lax.rem(place, 2)
    scale = 1.0 / math.sqrt(size)
    never = 4 * BLOCK
    own_gap = lax.broadcasted_iota(jnp.int32, (BLOCK, BLOCK), 0) - lax.broadcasted_iota(
        jnp.int32, (BLOCK, BLOCK), 1
    )
    own_gap = jnp.where(own_gap >= 0, own_gap, never)
    back_gap = lax.broadcasted_iota(jnp.int32, (BLOCK, HALO), 0) - lax.broadcasted_iota(
        jnp.int32, (BLOCK, HALO), 1
    )
    back_gap = jnp.where(place > 0, back_gap + HALO, never)
    far_chip = (lax.broadcasted_iota(jnp.int32, (BLOCK, far_rows), 1) // per_block) ^ chip
    mine_gap = jnp.where(far_chip * 2 + core < place, 0, never)
    other_gap = jnp.where(far_chip * 2 + (1 - core) < place, 0, never)
    gap = jnp.concatenate([own_gap, mine_gap, other_gap, back_gap], 1)
    some = 2 if heads % 2 == 0 else 1
    for first in range(0, heads, some):
        cols = slice(first * size, (first + some) * size)
        keys, values = [
            jnp.concatenate(
                [
                    own[:, cols],
                    mine_ref[:, part, :, cols].reshape(far_rows, some * size),
                    other_ref[:, part, :, cols].reshape(far_rows, some * size),
                    halo_ref[part, :, cols],
                ],
                0,
            )
            for part, own in enumerate((k_ref, v_ref))
        ]
        query = q_ref[:, cols]
        if some == 2:
            zero = jnp.zeros((BLOCK, size), BF16)
            query = jnp.concatenate(
                [
                    jnp.concatenate([query[:, :size], zero], 1),
                    jnp.concatenate([zero, query[:, size:]], 1),
                ],
                0,
            )
        scores = lax.dot_general(query, keys, LAST, preferred_element_type=jnp.float32) * scale
        rounded, totals = [], []
        for j in range(some):
            valid = gap < width_ref[first + j : first + j + 1, :]
            part = jnp.where(valid, scores[j * BLOCK : (j + 1) * BLOCK], NEGATIVE_FILL)
            largest = jnp.max(part, axis=1, keepdims=True)
            weights = jnp.where(valid, jnp.exp(part - largest), 0.0)
            totals.append(jnp.sum(weights, axis=1, keepdims=True))
            rounded.append(weights.astype(BF16))
        mixed = jnp.dot(jnp.concatenate(rounded, 0), values, preferred_element_type=jnp.float32)
        for j in range(some):
            own = slice((first + j) * size, (first + j + 1) * size)
            taken = mixed[j * BLOCK : (j + 1) * BLOCK, j * size : (j + 1) * size]
            out_ref[:, own] = (taken / totals[j]).astype(BF16)


def cut_kernel(first_ref, second_ref, *refs):
    low_ref, high_ref = refs[-2:]
    half = low_ref.shape[0]
    low_ref[...] = first_ref[:half]
    high_ref[...] = second_ref[half:]


def project_kernel(count, *refs):
    pieces, (mine_ref, other_ref) = refs[:count], refs[count : count + 2]
    send_ref, keep_ref = refs[-2:]
    core = lax.rem(lax.axis_index("seq"), 2)
    side = lax.rem(lax.axis_index("head"), 2)
    rows_in = []
    for parity in (1 - side, side):
        for ref in pieces:
            for j in range(ref.shape[0] // 2):
                rows_in.append(ref[2 * j + parity])
    rows_in = jnp.concatenate(rows_in, 0)
    for which, ref in ((core, mine_ref), (1 - core, other_ref)):
        found = lax.dot_general(rows_in, ref[...], LAST, preferred_element_type=jnp.float32)
        found = found.astype(BF16).reshape((2,) + send_ref.shape[1:])
        send_ref[which] = found[0]
        keep_ref[which] = found[1]


def project_first_kernel(att_ref, mine_ref, other_ref, passed_ref, send_ref, keep_ref):
    project_kernel(1, att_ref, mine_ref, other_ref, send_ref, keep_ref)


def split_kernel(came_ref, keep_ref, *refs):
    side = lax.axis_index("head") // 2
    n = came_ref.shape[1]
    for k in range(n):
        for ref, which in ((refs[-2 * n + 2 * k], 1 - side), (refs[-2 * n + 2 * k + 1], side)):
            total = came_ref[:, k, which].astype(jnp.float32) + keep_ref[:, k, which].astype(jnp.float32)
            ref[...] = total.astype(BF16)


def join_kernel(*refs):
    out_ref = refs[-1]
    wide = refs[0].shape[-1]
    chip = lax.axis_index("seq") // 2
    for k in range(len(refs) // 2):
        total = refs[2 * k][...].astype(jnp.float32) + refs[2 * k + 1][...].astype(jnp.float32)
        total = total.astype(BF16)
        if len(out_ref.shape) == 4:
            out_ref[chip ^ k] = total
            continue
        for c in range(2):
            start = pl.multiple_of((chip ^ k) * (2 * wide), 128)
            out_ref[:, pl.ds(start + c * wide, wide)] = total[c]


def local(queries, keys, values, band, picks, w_out):
    heads = band.shape[0]
    tok_rows, feat = queries.shape
    per_block = picks.shape[1]
    seq = lax.axis_size("seq")
    groups = lax.axis_size("head")
    wide = w_out.shape[0]
    rows = tok_rows // groups
    chips = seq // 2
    half = groups // 2

    def swap(value, k, z):
        if k == 0:
            return lax.ppermute(value, "head", [(i, i ^ z) for i in range(groups)])
        if z == 0:
            return lax.ppermute(value, "seq", [(i, i ^ k) for i in range(seq)])
        pairs = [
            (s * groups + h, (s ^ k) * groups + (h ^ z)) for s in range(seq) for h in range(groups)
        ]
        return lax.ppermute(value, ("seq", "head"), pairs)

    other_w = swap(w_out, 1, 0)
    listed = BLOCK + HALO + seq * per_block
    summary, halo, width, queries, keys, values = pl.pallas_call(
        pick_kernel,
        out_shape=(
            shaped(2, per_block, feat),
            shaped(2, HALO, feat),
            pltpu.VMEM((heads, listed), jnp.int32),
        )
        + (shaped(tok_rows, feat),) * 3,
        in_specs=[smem(), smem(), hbm(), hbm(), hbm()],
        out_specs=(vmem(),) * 6,
        scratch_shapes=[pltpu.SemaphoreType.DMA((3,))],
        compiler_params=PARAMS,
    )(*far_away(picks, band, queries, keys, values))
    far = [summary] + [swap(summary, 2 * k, 0) for k in range(1, chips)]
    halo = lax.ppermute(halo, "seq", [(i, i + 1) for i in range(seq - 1)])
    mine = pl.pallas_call(
        stack_kernel,
        out_shape=shaped(chips, 2, per_block, feat),
        in_specs=[vmem()] * chips,
        out_specs=vmem(),
        compiler_params=PARAMS,
    )(*far)
    other = swap(mine, 1, 0)
    attention = pl.pallas_call(
        attend_kernel,
        out_shape=shaped(tok_rows, feat),
        in_specs=[vmem()] * 7,
        out_specs=vmem(),
        compiler_params=PARAMS,
    )(width, queries, keys, values, halo, mine, other)
    attention = attention.reshape(groups, rows, feat)
    attention, send, keep = pl.pallas_call(
        project_first_kernel,
        out_shape=(shaped(groups, rows, feat),) + (shaped(2, 1, half, rows, wide),) * 2,
        in_specs=[vmem()] * 3,
        out_specs=(vmem(),) * 3,
        input_output_aliases={0: 0},
        compiler_params=PARAMS,
    )(attention, w_out, other_w)
    parts = {k: [swap(attention, 2 * k, 0)] for k in range(1, chips) if k != 3}
    found = {}

    def after(*arrays):
        return [pl.BlockSpec(memory_space=pl.ANY)] * len(arrays), arrays

    def projected(group, order):
        pieces = [piece for k in group for piece in parts[k]]
        n = len(group)
        specs, arrays = after(*order)
        return pl.pallas_call(
            functools.partial(project_kernel, len(pieces)),
            out_shape=(shaped(2, n, half, rows, wide),) * 2,
            in_specs=[vmem()] * (len(pieces) + 2) + specs,
            out_specs=(vmem(),) * 2,
            compiler_params=PARAMS,
        )(*pieces, w_out, other_w, *arrays)

    def exchanged(group, send, keep, order=()):
        came = swap(send, 0, 1)
        specs, arrays = after(*order)
        n = len(group)
        parted = pl.pallas_call(
            split_kernel,
            out_shape=(shaped(2, rows, wide),) * (2 * n),
            in_specs=[vmem()] * 2 + specs,
            out_specs=(vmem(),) * (2 * n),
            compiler_params=PARAMS,
        )(came, keep, *arrays)
        for k, away, stay in zip(group, parted[::2], parted[1::2]):
            found[k] = [swap(away, 2 * k, 2), swap(stay, 2 * k, 0) if k else stay]
        return parted

    first = exchanged([0], send, keep)
    pair = [k for k in (1, 2) if k < chips]
    if pair:
        send, keep = projected(pair, (first[1],))
        second = exchanged(pair, send, keep)
    if chips > 3:
        specs, arrays = after(keep, found[0][0])
        low, high = pl.pallas_call(
            cut_kernel,
            out_shape=(shaped(half, rows, feat),) * 2,
            in_specs=[vmem()] * 2 + specs,
            out_specs=(vmem(),) * 2,
            compiler_params=PARAMS,
        )(parts[1][0], parts[2][0], *arrays)
        parts[3] = [swap(low, 4, 0), swap(high, 2, 0)]
    for k in range(3, chips):
        exchanged([k], *projected([k], ()))
    flat = wide % 128 == 0
    joined = pl.pallas_call(
        join_kernel,
        out_shape=jax.ShapeDtypeStruct((rows, seq * wide) if flat else (chips, 2, rows, wide), BF16),
        in_specs=[vmem()] * (2 * chips),
        out_specs=vmem(),
        compiler_params=PARAMS,
    )(*[piece for k in range(chips) for piece in found[k]])
    return joined if flat else joined.transpose(2, 0, 1, 3).reshape(rows, seq * wide)


def solution(mesh):
    placed = (
        P("seq", "head"),
        P("seq", "head"),
        P("seq", "head"),
        P("head"),
        P("seq", None),
        P("seq", "head"),
    )
    return jax.shard_map(
        local, mesh=mesh, in_specs=placed, out_specs=P(("seq", "head"), None), check_vma=False
    )
```

```python
import functools
import math

import jax
import jax.numpy as jnp
from jax import lax
from jax.experimental import pallas as pl
from jax.experimental.pallas import tpu as pltpu
from jax.sharding import PartitionSpec as P

BLOCK = 128
HALO = 64
NEGATIVE_FILL = -1e30
LAST = (((1,), (1,)), ((), ()))
BF16 = jnp.bfloat16
BRIEF = pl.CostEstimate(flops=0, bytes_accessed=0, transcendentals=0)
LONGER = pl.CostEstimate(flops=1_100_000_000, bytes_accessed=3_000_000, transcendentals=0)
PARAMS = pltpu.CompilerParams(vmem_limit_bytes=32 << 20)


def vmem():
    return pl.BlockSpec(memory_space=pltpu.VMEM)


def smem():
    return pl.BlockSpec(memory_space=pltpu.SMEM)


def hbm():
    return pl.BlockSpec(memory_space=pltpu.HBM)


def shaped(*shape):
    return pltpu.VMEM(shape, BF16)


def far_away(*arrays):
    return [pltpu.with_memory_space_constraint(array, pltpu.HBM) for array in arrays]


def column_of(count, width, number):
    row = lax.broadcasted_iota(jnp.int32, (count, width), 0)
    found = jnp.zeros((count, width), jnp.int32)
    for r in range(count):
        found = jnp.where(row == r, number(r), found)
    return found


def pick_kernel(
    picks_ref, band_ref, q_hbm, k_hbm, v_hbm, summary_ref, halo_ref, width_ref, q_ref, k_ref, v_ref, sems
):
    per_block = picks_ref.shape[1]
    copies = [
        pltpu.make_async_copy(ref, into, sems.at[part])
        for part, (ref, into) in enumerate(((k_hbm, k_ref), (v_hbm, v_ref), (q_hbm, q_ref)))
    ]
    for copy in copies:
        copy.start()
    wanted = column_of(per_block, BLOCK, lambda r: picks_ref[0, r])
    width_ref[...] = column_of(*width_ref.shape, lambda r: band_ref[r])
    column = lax.broadcasted_iota(jnp.int32, (per_block, BLOCK), 1)
    chosen = jnp.where(column == wanted, 1.0, 0.0).astype(BF16)
    for part, ref in enumerate((k_ref, v_ref)):
        copies[part].wait()
        taken = jnp.dot(chosen, ref[...], preferred_element_type=jnp.float32)
        summary_ref[part] = taken.astype(BF16)
        halo_ref[part] = ref[BLOCK - HALO :, :]
    copies[2].wait()


def stack_kernel(*refs):
    for k, ref in enumerate(refs[:-1]):
        refs[-1][k] = ref[...]


def attend_kernel(low, width_ref, q_ref, k_ref, v_ref, *refs):
    halo_ref, mine_ref, other_ref = (refs if low else (None,) + refs)[:3]
    out_ref = refs[-1]
    size = BLOCK
    heads = q_ref.shape[1] // size
    start, count = (0, HALO) if low else (HALO, BLOCK - HALO)
    reach = start + count
    chips, unused, per_block, unused = mine_ref.shape
    far_rows = chips * per_block
    place = lax.axis_index("seq")
    chip = place // 2
    core = lax.rem(place, 2)
    scale = 1.0 / math.sqrt(size)
    never = 4 * BLOCK

    def distance(columns):
        row = lax.broadcasted_iota(jnp.int32, (count, columns), 0) + start
        return row - lax.broadcasted_iota(jnp.int32, (count, columns), 1)

    gap = distance(reach)
    gaps = [jnp.where(gap >= 0, gap, never)]
    if low:
        gaps.append(jnp.where(place > 0, distance(HALO) + HALO, never))
    far_chip = (lax.broadcasted_iota(jnp.int32, (count, far_rows), 1) // per_block) ^ chip
    gaps.append(jnp.where(far_chip * 2 + core < place, 0, never))
    gaps.append(jnp.where(far_chip * 2 + (1 - core) < place, 0, never))
    gap = jnp.concatenate(gaps, 1)
    listed = gap.shape[1]
    some = 2 if heads % 2 == 0 else 1
    for first in range(0, heads, some):
        cols = slice(first * size, (first + some) * size)
        keys, values = [
            jnp.concatenate(
                [own[:reach, cols]]
                + ([halo_ref[part, :, cols]] if low else [])
                + [ref[:, part, :, cols].reshape(far_rows, some * size) for ref in (mine_ref, other_ref)],
                0,
            )
            for part, own in enumerate((k_ref, v_ref))
        ]
        query = q_ref[start:reach, cols]
        if some == 2:
            zero = jnp.zeros((count, size), BF16)
            query = jnp.concatenate(
                [
                    jnp.concatenate([query[:, :size], zero], 1),
                    jnp.concatenate([zero, query[:, size:]], 1),
                ],
                0,
            )
        scores = lax.dot_general(query, keys, LAST, preferred_element_type=jnp.float32) * scale
        rounded, totals = [], []
        for j in range(some):
            valid = gap < width_ref[first + j : first + j + 1, :listed]
            part = jnp.where(valid, scores[j * count : (j + 1) * count], NEGATIVE_FILL)
            largest = jnp.max(part, axis=1, keepdims=True)
            weights = jnp.where(valid, jnp.exp(part - largest), 0.0)
            totals.append(jnp.sum(weights, axis=1, keepdims=True))
            rounded.append(weights.astype(BF16))
        mixed = jnp.dot(jnp.concatenate(rounded, 0), values, preferred_element_type=jnp.float32)
        for j in range(some):
            own = slice((first + j) * size, (first + j + 1) * size)
            taken = mixed[j * count : (j + 1) * count, j * size : (j + 1) * size]
            out_ref[:, own] = (taken / totals[j]).astype(BF16)


def project_kernel(high_ref, low_ref, mine_ref, other_ref, *refs):
    send_ref, keep_ref = refs[-2:]
    core = lax.rem(lax.axis_index("seq"), 2)
    side = lax.rem(lax.axis_index("head"), 2)
    rows_in = jnp.concatenate([ref[part] for part in (1 - side, side) for ref in (high_ref, low_ref)], 0)
    for which, ref in ((core, mine_ref), (1 - core, other_ref)):
        found = lax.dot_general(rows_in, ref[...], LAST, preferred_element_type=jnp.float32)
        found = found.astype(BF16).reshape((2,) + send_ref.shape[1:])
        send_ref[which] = found[0]
        keep_ref[which] = found[1]


def split_kernel(came_ref, keep_ref, *refs):
    away_ref, stay_ref = refs[-2:]
    side = lax.axis_index("head") // 2
    for ref, which in ((away_ref, side), (stay_ref, 1 - side)):
        total = came_ref[:, which].astype(jnp.float32) + keep_ref[:, which].astype(jnp.float32)
        ref[...] = total.astype(BF16)


def join_kernel(chunks, *refs):
    out_ref = refs[-1]
    wide = refs[0].shape[-1]
    chip = lax.axis_index("seq") // 2
    upper = lax.axis_index("head") // 2
    for n, (high, low) in enumerate(chunks):
        total = refs[2 * n][...].astype(jnp.float32) + refs[2 * n + 1][...].astype(jnp.float32)
        total = total.astype(BF16)
        source = chip ^ (high if high == low else jnp.where(upper == 1, high, low))
        if len(out_ref.shape) == 4:
            out_ref[source] = total
            continue
        for c in range(2):
            start = pl.multiple_of(source * (2 * wide), 128)
            out_ref[:, pl.ds(start + c * wide, wide)] = total[c]


def order_of_projection(n, keeps, stays, found):
    if n == 3:
        return [keeps[2], stays[1], found[0][0]]
    return [keeps[n - 1]] if 0 < n < 3 else []


def order_of_split(n, found):
    return [found[1][1]] if n in (2, 3) else []


def local(queries, keys, values, band, picks, w_out):
    heads = band.shape[0]
    tok_rows, feat = queries.shape
    per_block = picks.shape[1]
    seq = lax.axis_size("seq")
    groups = lax.axis_size("head")
    wide = w_out.shape[0]
    rows = tok_rows // groups
    chips = seq // 2
    half = groups // 2

    def swap(value, k, z):
        if k == 0:
            return lax.ppermute(value, "head", [(i, i ^ z) for i in range(groups)])
        if z == 0:
            return lax.ppermute(value, "seq", [(i, i ^ k) for i in range(seq)])
        pairs = [
            (s * groups + h, (s ^ k) * groups + (h ^ z)) for s in range(seq) for h in range(groups)
        ]
        return lax.ppermute(value, ("seq", "head"), pairs)

    other_w = swap(w_out, 1, 0)
    listed = BLOCK + seq * per_block
    summary, halo, width, queries, keys, values = pl.pallas_call(
        pick_kernel,
        out_shape=(
            shaped(2, per_block, feat),
            shaped(2, HALO, feat),
            pltpu.VMEM((heads, listed), jnp.int32),
        )
        + (shaped(tok_rows, feat),) * 3,
        in_specs=[smem(), smem(), hbm(), hbm(), hbm()],
        out_specs=(vmem(),) * 6,
        scratch_shapes=[pltpu.SemaphoreType.DMA((3,))],
        compiler_params=PARAMS,
    )(*far_away(picks, band, queries, keys, values))
    far = [summary] + [swap(summary, 2 * k, 0) for k in range(1, chips)]
    halo = lax.ppermute(halo, "seq", [(i, i + 1) for i in range(seq - 1)])
    mine = pl.pallas_call(
        stack_kernel,
        out_shape=shaped(chips, 2, per_block, feat),
        in_specs=[vmem()] * chips,
        out_specs=vmem(),
        compiler_params=PARAMS,
    )(*far)
    other = swap(mine, 1, 0)

    def attended(low, behind, order=()):
        return pl.pallas_call(
            functools.partial(attend_kernel, low),
            out_shape=shaped(HALO if low else tok_rows - HALO, feat),
            in_specs=[vmem()] * (6 + len(behind)) + [pl.BlockSpec(memory_space=pl.ANY)] * len(order),
            out_specs=vmem(),
            compiler_params=PARAMS,
            cost_estimate=LONGER,
        )(width, queries, keys, values, *behind, mine, other, *order).reshape(half, rows, feat)

    highs = [attended(False, (), (halo,))]
    lows = [attended(True, (halo,), ())]
    for k in range(1, chips):
        if k == 3:
            highs.append(swap(highs[1], 4, 0))
            lows.append(swap(lows[2], 2, 0))
            continue
        highs.append(swap(highs[0], 2 * k, 0))
        lows.append(swap(lows[0], 2 * k, 0))
    chunks = [(0, 0)] + [(1, 2), (2, 1)][: 2 if chips > 2 else 0] + ([(1, 1)] if chips == 2 else [])
    chunks += [(k, k) for k in range(3, chips)]

    def after(*arrays):
        return [pl.BlockSpec(memory_space=pl.ANY)] * len(arrays), arrays

    def projected(high, low, order):
        specs, arrays = after(*order)
        return pl.pallas_call(
            project_kernel,
            out_shape=(shaped(2, half, rows, wide),) * 2,
            in_specs=[vmem()] * 4 + specs,
            out_specs=(vmem(),) * 2,
            compiler_params=PARAMS,
            cost_estimate=BRIEF,
        )(highs[high], lows[low], w_out, other_w, *arrays)

    def owned(value, high, low, leaves):
        if not leaves and high == low == 0:
            return value
        pairs = []
        for s in range(seq):
            for h in range(groups):
                k = low if (h >= half) == leaves else high
                pairs.append((s * groups + h, (s ^ 2 * k) * groups + (h ^ 2 * leaves)))
        return lax.ppermute(value, ("seq", "head"), pairs)

    sends, keeps, aways, stays, found = {}, {}, {}, {}, {}
    for n, (high, low) in enumerate(chunks):
        sends[n], keeps[n] = projected(high, low, order_of_projection(n, keeps, stays, found))
        came = swap(sends[n], 0, 1)
        specs, arrays = after(*order_of_split(n, found))
        aways[n], stays[n] = pl.pallas_call(
            split_kernel,
            out_shape=(shaped(2, rows, wide),) * 2,
            in_specs=[vmem()] * 2 + specs,
            out_specs=(vmem(),) * 2,
            compiler_params=PARAMS,
        )(came, keeps[n], *arrays)
        found[n] = (owned(aways[n], high, low, True), owned(stays[n], high, low, False))
    flat = wide % 128 == 0
    joined = pl.pallas_call(
        functools.partial(join_kernel, chunks),
        out_shape=jax.ShapeDtypeStruct((rows, seq * wide) if flat else (chips, 2, rows, wide), BF16),
        in_specs=[vmem()] * (2 * chips),
        out_specs=vmem(),
        compiler_params=PARAMS,
    )(*[piece for n in range(chips) for piece in found[n]])
    return joined if flat else joined.transpose(2, 0, 1, 3).reshape(rows, seq * wide)


def solution(mesh):
    placed = (
        P("seq", "head"),
        P("seq", "head"),
        P("seq", "head"),
        P("head"),
        P("seq", None),
        P("seq", "head"),
    )
    return jax.shard_map(
        local, mesh=mesh, in_specs=placed, out_specs=P(("seq", "head"), None), check_vma=False
    )
```

```python
import functools
import math

import jax
import jax.numpy as jnp
from jax import lax
from jax.experimental import pallas as pl
from jax.experimental.pallas import tpu as pltpu
from jax.sharding import PartitionSpec as P

BLOCK = 128
HALO = 64
NEGATIVE_FILL = -1e30
LAST = (((1,), (1,)), ((), ()))
BF16 = jnp.bfloat16
BRIEF = pl.CostEstimate(flops=0, bytes_accessed=0, transcendentals=0)
LONGER = pl.CostEstimate(flops=1_100_000_000, bytes_accessed=3_000_000, transcendentals=0)
PARAMS = pltpu.CompilerParams(vmem_limit_bytes=32 << 20)


def vmem():
    return pl.BlockSpec(memory_space=pltpu.VMEM)


def smem():
    return pl.BlockSpec(memory_space=pltpu.SMEM)


def hbm():
    return pl.BlockSpec(memory_space=pltpu.HBM)


def shaped(*shape):
    return pltpu.VMEM(shape, BF16)


def far_away(*arrays):
    return [pltpu.with_memory_space_constraint(array, pltpu.HBM) for array in arrays]


def column_of(count, width, number):
    row = lax.broadcasted_iota(jnp.int32, (count, width), 0)
    found = jnp.zeros((count, width), jnp.int32)
    for r in range(count):
        found = jnp.where(row == r, number(r), found)
    return found


def pick_kernel(
    picks_ref, band_ref, q_hbm, k_hbm, v_hbm, summary_ref, halo_ref, width_ref, q_ref, k_ref, v_ref, sems
):
    per_block = picks_ref.shape[1]
    copies = [
        pltpu.make_async_copy(ref, into, sems.at[part])
        for part, (ref, into) in enumerate(((k_hbm, k_ref), (v_hbm, v_ref), (q_hbm, q_ref)))
    ]
    for copy in copies:
        copy.start()
    wanted = column_of(per_block, BLOCK, lambda r: picks_ref[0, r])
    width_ref[...] = column_of(*width_ref.shape, lambda r: band_ref[r])
    column = lax.broadcasted_iota(jnp.int32, (per_block, BLOCK), 1)
    chosen = jnp.where(column == wanted, 1.0, 0.0).astype(BF16)
    for part, ref in enumerate((k_ref, v_ref)):
        copies[part].wait()
        taken = jnp.dot(chosen, ref[...], preferred_element_type=jnp.float32)
        summary_ref[part] = taken.astype(BF16)
        halo_ref[part] = ref[BLOCK - HALO :, :]
    copies[2].wait()


def stack_kernel(*refs):
    for k, ref in enumerate(refs[:-1]):
        refs[-1][k] = ref[...]


def attend_kernel(low, width_ref, q_ref, k_ref, v_ref, *refs):
    halo_ref, mine_ref, other_ref = (refs if low else (None,) + refs)[:3]
    out_ref = refs[-1]
    size = BLOCK
    heads = q_ref.shape[1] // size
    start, count = (0, HALO) if low else (HALO, BLOCK - HALO)
    reach = start + count
    chips, unused, per_block, unused = mine_ref.shape
    far_rows = chips * per_block
    place = lax.axis_index("seq")
    chip = place // 2
    core = lax.rem(place, 2)
    scale = 1.0 / math.sqrt(size)
    never = 4 * BLOCK

    def distance(columns):
        row = lax.broadcasted_iota(jnp.int32, (count, columns), 0) + start
        return row - lax.broadcasted_iota(jnp.int32, (count, columns), 1)

    gap = distance(reach)
    gaps = [jnp.where(gap >= 0, gap, never)]
    if low:
        gaps.append(jnp.where(place > 0, distance(HALO) + HALO, never))
    far_chip = (lax.broadcasted_iota(jnp.int32, (count, far_rows), 1) // per_block) ^ chip
    gaps.append(jnp.where(far_chip * 2 + core < place, 0, never))
    gaps.append(jnp.where(far_chip * 2 + (1 - core) < place, 0, never))
    gap = jnp.concatenate(gaps, 1)
    listed = gap.shape[1]
    some = 2 if heads % 2 == 0 else 1
    starts = range(0, heads, some)

    def listing(part, own, first):
        cols = slice(first * size, (first + some) * size)
        return jnp.concatenate(
            [own[:reach, cols]]
            + ([halo_ref[part, :, cols]] if low else [])
            + [ref[:, part, :, cols].reshape(far_rows, some * size) for ref in (mine_ref, other_ref)],
            0,
        )

    scores = []
    for first in starts:
        query = q_ref[start:reach, first * size : (first + some) * size]
        if some == 2:
            zero = jnp.zeros((count, size), BF16)
            query = jnp.concatenate(
                [
                    jnp.concatenate([query[:, :size], zero], 1),
                    jnp.concatenate([zero, query[:, size:]], 1),
                ],
                0,
            )
        scores.append(
            lax.dot_general(query, listing(0, k_ref, first), LAST, preferred_element_type=jnp.float32)
        )
    weights, totals = [], []
    for h in range(heads):
        valid = gap < width_ref[h : h + 1, :listed]
        rows = slice(h % some * count, (h % some + 1) * count)
        part = jnp.where(valid, scores[h // some][rows] * scale, NEGATIVE_FILL)
        largest = jnp.max(part, axis=1, keepdims=True)
        part = jnp.where(valid, jnp.exp(part - largest), 0.0)
        totals.append(jnp.sum(part, axis=1, keepdims=True))
        weights.append(part.astype(BF16))
    for first in starts:
        rounded = jnp.concatenate(weights[first : first + some], 0)
        mixed = jnp.dot(rounded, listing(1, v_ref, first), preferred_element_type=jnp.float32)
        for j in range(some):
            taken = mixed[j * count : (j + 1) * count, j * size : (j + 1) * size]
            out_ref[:, (first + j) * size : (first + j + 1) * size] = (taken / totals[first + j]).astype(BF16)


def project_kernel(high_ref, low_ref, mine_ref, other_ref, *refs):
    send_ref, keep_ref = refs[-2:]
    core = lax.rem(lax.axis_index("seq"), 2)
    side = lax.rem(lax.axis_index("head"), 2)
    rows_in = [ref[part] for part in (1 - side, side) for ref in (high_ref, low_ref)]
    rows_in = jnp.concatenate(rows_in * 2, 0)
    for which, ref in ((core, mine_ref), (1 - core, other_ref)):
        found = lax.dot_general(rows_in, ref[...], LAST, preferred_element_type=jnp.float32)
        found = found[: rows_in.shape[0] // 2].astype(BF16).reshape((2,) + send_ref.shape[1:])
        send_ref[which] = found[0]
        keep_ref[which] = found[1]


def split_kernel(came_ref, keep_ref, *refs):
    away_ref, stay_ref = refs[-2:]
    side = lax.axis_index("head") // 2
    for ref, which in ((away_ref, side), (stay_ref, 1 - side)):
        total = came_ref[:, which].astype(jnp.float32) + keep_ref[:, which].astype(jnp.float32)
        ref[...] = total.astype(BF16)


def join_kernel(chunks, *refs):
    out_ref = refs[-1]
    wide = refs[0].shape[-1]
    chip = lax.axis_index("seq") // 2
    upper = lax.axis_index("head") // 2
    for n, (high, low) in enumerate(chunks):
        total = refs[2 * n][...].astype(jnp.float32) + refs[2 * n + 1][...].astype(jnp.float32)
        total = total.astype(BF16)
        source = chip ^ (high if high == low else jnp.where(upper == 1, high, low))
        if len(out_ref.shape) == 4:
            out_ref[source] = total
            continue
        for c in range(2):
            start = pl.multiple_of(source * (2 * wide), 128)
            out_ref[:, pl.ds(start + c * wide, wide)] = total[c]


def order_of_projection(n, keeps, stays, found):
    if n == 3:
        return [keeps[2], stays[1], found[0][0]]
    return [keeps[n - 1]] if 0 < n < 3 else []


def order_of_split(n, found):
    return [found[1][1]] if n in (2, 3) else []


def local(queries, keys, values, band, picks, w_out):
    heads = band.shape[0]
    tok_rows, feat = queries.shape
    per_block = picks.shape[1]
    seq = lax.axis_size("seq")
    groups = lax.axis_size("head")
    wide = w_out.shape[0]
    rows = tok_rows // groups
    chips = seq // 2
    half = groups // 2

    def swap(value, k, z):
        if k == 0:
            return lax.ppermute(value, "head", [(i, i ^ z) for i in range(groups)])
        if z == 0:
            return lax.ppermute(value, "seq", [(i, i ^ k) for i in range(seq)])
        pairs = [
            (s * groups + h, (s ^ k) * groups + (h ^ z)) for s in range(seq) for h in range(groups)
        ]
        return lax.ppermute(value, ("seq", "head"), pairs)

    other_w = swap(w_out, 1, 0)
    listed = BLOCK + seq * per_block
    summary, halo, width, queries, keys, values = pl.pallas_call(
        pick_kernel,
        out_shape=(
            shaped(2, per_block, feat),
            shaped(2, HALO, feat),
            pltpu.VMEM((heads, listed), jnp.int32),
        )
        + (shaped(tok_rows, feat),) * 3,
        in_specs=[smem(), smem(), hbm(), hbm(), hbm()],
        out_specs=(vmem(),) * 6,
        scratch_shapes=[pltpu.SemaphoreType.DMA((3,))],
        compiler_params=PARAMS,
    )(*far_away(picks, band, queries, keys, values))
    far = [summary] + [swap(summary, 2 * k, 0) for k in range(1, chips)]
    halo = lax.ppermute(halo, "seq", [(i, i + 1) for i in range(seq - 1)])
    mine = pl.pallas_call(
        stack_kernel,
        out_shape=shaped(chips, 2, per_block, feat),
        in_specs=[vmem()] * chips,
        out_specs=vmem(),
        compiler_params=PARAMS,
    )(*far)
    other = swap(mine, 1, 0)

    def attended(low, behind, order=()):
        return pl.pallas_call(
            functools.partial(attend_kernel, low),
            out_shape=shaped(HALO if low else tok_rows - HALO, feat),
            in_specs=[vmem()] * (6 + len(behind)) + [pl.BlockSpec(memory_space=pl.ANY)] * len(order),
            out_specs=vmem(),
            compiler_params=PARAMS,
            cost_estimate=LONGER,
        )(width, queries, keys, values, *behind, mine, other, *order).reshape(half, rows, feat)

    highs = [attended(False, (), (halo,))]
    lows = [attended(True, (halo,), ())]
    for k in range(1, chips):
        if k == 3:
            highs.append(swap(highs[1], 4, 0))
            lows.append(swap(lows[2], 2, 0))
            continue
        highs.append(swap(highs[0], 2 * k, 0))
        lows.append(swap(lows[0], 2 * k, 0))
    chunks = [(0, 0)] + [(1, 2), (2, 1)][: 2 if chips > 2 else 0] + ([(1, 1)] if chips == 2 else [])
    chunks += [(k, k) for k in range(3, chips)]

    def after(*arrays):
        return [pl.BlockSpec(memory_space=pl.ANY)] * len(arrays), arrays

    def projected(high, low, order):
        specs, arrays = after(*order)
        return pl.pallas_call(
            project_kernel,
            out_shape=(shaped(2, half, rows, wide),) * 2,
            in_specs=[vmem()] * 4 + specs,
            out_specs=(vmem(),) * 2,
            compiler_params=PARAMS,
            cost_estimate=BRIEF,
        )(highs[high], lows[low], w_out, other_w, *arrays)

    def owned(value, high, low, leaves):
        if not leaves and high == low == 0:
            return value
        pairs = []
        for s in range(seq):
            for h in range(groups):
                k = low if (h >= half) == leaves else high
                pairs.append((s * groups + h, (s ^ 2 * k) * groups + (h ^ 2 * leaves)))
        return lax.ppermute(value, ("seq", "head"), pairs)

    sends, keeps, aways, stays, found = {}, {}, {}, {}, {}
    for n, (high, low) in enumerate(chunks):
        sends[n], keeps[n] = projected(high, low, order_of_projection(n, keeps, stays, found))
        came = swap(sends[n], 0, 1)
        specs, arrays = after(*order_of_split(n, found))
        aways[n], stays[n] = pl.pallas_call(
            split_kernel,
            out_shape=(shaped(2, rows, wide),) * 2,
            in_specs=[vmem()] * 2 + specs,
            out_specs=(vmem(),) * 2,
            compiler_params=PARAMS,
        )(came, keeps[n], *arrays)
        found[n] = (owned(aways[n], high, low, True), owned(stays[n], high, low, False))
    flat = wide % 128 == 0
    joined = pl.pallas_call(
        functools.partial(join_kernel, chunks),
        out_shape=jax.ShapeDtypeStruct((rows, seq * wide) if flat else (chips, 2, rows, wide), BF16),
        in_specs=[vmem()] * (2 * chips),
        out_specs=vmem(),
        compiler_params=PARAMS,
    )(*[piece for n in range(chips) for piece in found[n]])
    return joined if flat else joined.transpose(2, 0, 1, 3).reshape(rows, seq * wide)


def solution(mesh):
    placed = (
        P("seq", "head"),
        P("seq", "head"),
        P("seq", "head"),
        P("head"),
        P("seq", None),
        P("seq", "head"),
    )
    return jax.shard_map(
        local, mesh=mesh, in_specs=placed, out_specs=P(("seq", "head"), None), check_vma=False
    )
```

```python
import functools
import math

import jax
import jax.numpy as jnp
from jax import lax
from jax.experimental import pallas as pl
from jax.experimental.pallas import tpu as pltpu
from jax.sharding import PartitionSpec as P

BLOCK = 128
HALO = 64
NEGATIVE_FILL = -1e30
LAST = (((1,), (1,)), ((), ()))
BF16 = jnp.bfloat16
BRIEF = pl.CostEstimate(flops=0, bytes_accessed=0, transcendentals=0)
LONGER = pl.CostEstimate(flops=1_100_000_000, bytes_accessed=3_000_000, transcendentals=0)
PARAMS = pltpu.CompilerParams(vmem_limit_bytes=32 << 20)


def vmem():
    return pl.BlockSpec(memory_space=pltpu.VMEM)


def smem():
    return pl.BlockSpec(memory_space=pltpu.SMEM)


def hbm():
    return pl.BlockSpec(memory_space=pltpu.HBM)


def shaped(*shape):
    return pltpu.VMEM(shape, BF16)


def far_away(*arrays):
    return [pltpu.with_memory_space_constraint(array, pltpu.HBM) for array in arrays]


def column_of(count, width, number):
    row = lax.broadcasted_iota(jnp.int32, (count, width), 0)
    found = jnp.zeros((count, width), jnp.int32)
    for r in range(count):
        found = jnp.where(row == r, number(r), found)
    return found


def pick_kernel(
    picks_ref, band_ref, q_hbm, k_hbm, v_hbm, summary_ref, halo_ref, width_ref, q_ref, k_ref, v_ref, sems
):
    per_block = picks_ref.shape[1]
    copies = [
        pltpu.make_async_copy(ref, into, sems.at[part])
        for part, (ref, into) in enumerate(((k_hbm, k_ref), (v_hbm, v_ref), (q_hbm, q_ref)))
    ]
    for copy in copies:
        copy.start()
    wanted = column_of(per_block, BLOCK, lambda r: picks_ref[0, r])
    width_ref[...] = column_of(*width_ref.shape, lambda r: band_ref[r])
    column = lax.broadcasted_iota(jnp.int32, (per_block, BLOCK), 1)
    chosen = jnp.where(column == wanted, 1.0, 0.0).astype(BF16)
    for part, ref in enumerate((k_ref, v_ref)):
        copies[part].wait()
        taken = jnp.dot(chosen, ref[...], preferred_element_type=jnp.float32)
        summary_ref[part] = taken.astype(BF16)
        halo_ref[part] = ref[BLOCK - HALO :, :]
    copies[2].wait()


def stack_kernel(*refs):
    for k, ref in enumerate(refs[:-1]):
        refs[-1][k] = ref[...]


def attend_kernel(low, width_ref, q_ref, k_ref, v_ref, *refs):
    halo_ref, mine_ref, other_ref = (refs if low else (None,) + refs)[:3]
    out_ref = refs[-1]
    size = BLOCK
    heads = q_ref.shape[1] // size
    start, count = (0, HALO) if low else (HALO, BLOCK - HALO)
    reach = start + count
    chips, unused, per_block, unused = mine_ref.shape
    far_rows = chips * per_block
    place = lax.axis_index("seq")
    chip = place // 2
    core = lax.rem(place, 2)
    scale = 1.0 / math.sqrt(size)
    never = 4 * BLOCK

    def distance(columns):
        row = lax.broadcasted_iota(jnp.int32, (count, columns), 0) + start
        return row - lax.broadcasted_iota(jnp.int32, (count, columns), 1)

    gap = distance(reach)
    gaps = [jnp.where(gap >= 0, gap, never)]
    if low:
        gaps.append(jnp.where(place > 0, distance(HALO) + HALO, never))
    far_chip = (lax.broadcasted_iota(jnp.int32, (count, far_rows), 1) // per_block) ^ chip
    gaps.append(jnp.where(far_chip * 2 + core < place, 0, never))
    gaps.append(jnp.where(far_chip * 2 + (1 - core) < place, 0, never))
    gap = jnp.concatenate(gaps, 1)
    listed = gap.shape[1]
    some = 2 if heads % 2 == 0 else 1
    starts = range(0, heads, some)

    def listing(part, own, first):
        cols = slice(first * size, (first + some) * size)
        return jnp.concatenate(
            [own[:reach, cols]]
            + ([halo_ref[part, :, cols]] if low else [])
            + [ref[:, part, :, cols].reshape(far_rows, some * size) for ref in (mine_ref, other_ref)],
            0,
        )

    scores = []
    for first in starts:
        query = q_ref[start:reach, first * size : (first + some) * size]
        if some == 2:
            zero = jnp.zeros((count, size), BF16)
            query = jnp.concatenate(
                [
                    jnp.concatenate([query[:, :size], zero], 1),
                    jnp.concatenate([zero, query[:, size:]], 1),
                ],
                0,
            )
        scores.append(
            lax.dot_general(query, listing(0, k_ref, first), LAST, preferred_element_type=jnp.float32)
        )
    weights, totals = [], []
    for h in range(heads):
        valid = gap < width_ref[h : h + 1, :listed]
        rows = slice(h % some * count, (h % some + 1) * count)
        part = jnp.where(valid, scores[h // some][rows] * scale, NEGATIVE_FILL)
        largest = jnp.max(part, axis=1, keepdims=True)
        part = jnp.where(valid, jnp.exp(part - largest), 0.0)
        totals.append(jnp.sum(part, axis=1, keepdims=True))
        weights.append(part.astype(BF16))
    for first in starts:
        rounded = jnp.concatenate(weights[first : first + some], 0)
        mixed = jnp.dot(rounded, listing(1, v_ref, first), preferred_element_type=jnp.float32)
        for j in range(some):
            taken = mixed[j * count : (j + 1) * count, j * size : (j + 1) * size]
            out_ref[:, (first + j) * size : (first + j + 1) * size] = (taken / totals[first + j]).astype(BF16)


def turn_kernel(mine_hbm, other_ref, order_ref, out_ref, mine_ref, sem):
    core = lax.rem(lax.axis_index("seq"), 2)
    wide = mine_ref.shape[0]
    step = math.gcd(wide, 128)
    copy = pltpu.make_async_copy(mine_hbm, mine_ref, sem)
    copy.start()
    for which, ref in ((1 - core, other_ref), (core, mine_ref)):
        if ref is mine_ref:
            copy.wait()
        for n in range(0, wide, step):
            out_ref[which, :, n : n + step] = ref[n : n + step, :].T


def project_kernel(high_ref, low_ref, turned_ref, *refs):
    send_ref, keep_ref = refs[-2:]
    side = lax.rem(lax.axis_index("head"), 2)
    rows_in = [ref[part] for part in (1 - side, side) for ref in (high_ref, low_ref)]
    rows_in = jnp.concatenate(rows_in, 0)
    for which in range(2):
        found = jnp.dot(rows_in, turned_ref[which], preferred_element_type=jnp.float32)
        found = found.astype(BF16).reshape((2,) + send_ref.shape[1:])
        send_ref[which] = found[0]
        keep_ref[which] = found[1]


def split_kernel(came_ref, keep_ref, *refs):
    away_ref, stay_ref = refs[-2:]
    side = lax.axis_index("head") // 2
    for ref, which in ((away_ref, side), (stay_ref, 1 - side)):
        total = came_ref[:, which].astype(jnp.float32) + keep_ref[:, which].astype(jnp.float32)
        ref[...] = total.astype(BF16)


def join_kernel(chunks, *refs):
    out_ref = refs[-1]
    wide = refs[0].shape[-1]
    chip = lax.axis_index("seq") // 2
    upper = lax.axis_index("head") // 2
    for n, (high, low) in enumerate(chunks):
        total = refs[2 * n][...].astype(jnp.float32) + refs[2 * n + 1][...].astype(jnp.float32)
        total = total.astype(BF16)
        source = chip ^ (high if high == low else jnp.where(upper == 1, high, low))
        if len(out_ref.shape) == 4:
            out_ref[source] = total
            continue
        for c in range(2):
            start = pl.multiple_of(source * (2 * wide), 128)
            out_ref[:, pl.ds(start + c * wide, wide)] = total[c]


def order_of_projection(n, keeps, stays, found):
    if n == 3:
        return [keeps[2], stays[1], found[0][0]]
    return [keeps[n - 1]] if 0 < n < 3 else []


def order_of_split(n, found):
    return [found[1][1]] if n in (2, 3) else []


def local(queries, keys, values, band, picks, w_out):
    heads = band.shape[0]
    tok_rows, feat = queries.shape
    per_block = picks.shape[1]
    seq = lax.axis_size("seq")
    groups = lax.axis_size("head")
    wide = w_out.shape[0]
    rows = tok_rows // groups
    chips = seq // 2
    half = groups // 2

    def swap(value, k, z):
        if k == 0:
            return lax.ppermute(value, "head", [(i, i ^ z) for i in range(groups)])
        if z == 0:
            return lax.ppermute(value, "seq", [(i, i ^ k) for i in range(seq)])
        pairs = [
            (s * groups + h, (s ^ k) * groups + (h ^ z)) for s in range(seq) for h in range(groups)
        ]
        return lax.ppermute(value, ("seq", "head"), pairs)

    other_w = swap(w_out, 1, 0)
    listed = BLOCK + seq * per_block
    summary, halo, width, queries, keys, values = pl.pallas_call(
        pick_kernel,
        out_shape=(
            shaped(2, per_block, feat),
            shaped(2, HALO, feat),
            pltpu.VMEM((heads, listed), jnp.int32),
        )
        + (shaped(tok_rows, feat),) * 3,
        in_specs=[smem(), smem(), hbm(), hbm(), hbm()],
        out_specs=(vmem(),) * 6,
        scratch_shapes=[pltpu.SemaphoreType.DMA((3,))],
        compiler_params=PARAMS,
    )(*far_away(picks, band, queries, keys, values))
    far = [summary] + [swap(summary, 2 * k, 0) for k in range(1, chips)]
    halo = lax.ppermute(halo, "seq", [(i, i + 1) for i in range(seq - 1)])
    mine = pl.pallas_call(
        stack_kernel,
        out_shape=shaped(chips, 2, per_block, feat),
        in_specs=[vmem()] * chips,
        out_specs=vmem(),
        compiler_params=PARAMS,
    )(*far)
    other = swap(mine, 1, 0)
    turned = pl.pallas_call(
        turn_kernel,
        out_shape=shaped(2, feat, wide),
        in_specs=[hbm(), vmem(), pl.BlockSpec(memory_space=pl.ANY)],
        out_specs=vmem(),
        scratch_shapes=[pltpu.VMEM((wide, feat), BF16), pltpu.SemaphoreType.DMA(())],
        compiler_params=PARAMS,
    )(*far_away(w_out), other_w, mine)

    def attended(low, behind, order=()):
        return pl.pallas_call(
            functools.partial(attend_kernel, low),
            out_shape=shaped(HALO if low else tok_rows - HALO, feat),
            in_specs=[vmem()] * (6 + len(behind)) + [pl.BlockSpec(memory_space=pl.ANY)] * len(order),
            out_specs=vmem(),
            compiler_params=PARAMS,
            cost_estimate=LONGER,
        )(width, queries, keys, values, *behind, mine, other, *order).reshape(half, rows, feat)

    highs = [attended(False, (), (halo, turned))]
    lows = [attended(True, (halo,), (turned,))]
    for k in range(1, chips):
        if k == 3:
            highs.append(swap(highs[1], 4, 0))
            lows.append(swap(lows[2], 2, 0))
            continue
        highs.append(swap(highs[0], 2 * k, 0))
        lows.append(swap(lows[0], 2 * k, 0))
    chunks = [(0, 0)] + [(1, 2), (2, 1)][: 2 if chips > 2 else 0] + ([(1, 1)] if chips == 2 else [])
    chunks += [(k, k) for k in range(3, chips)]

    def after(*arrays):
        return [pl.BlockSpec(memory_space=pl.ANY)] * len(arrays), arrays

    def projected(high, low, order):
        specs, arrays = after(*order)
        return pl.pallas_call(
            project_kernel,
            out_shape=(shaped(2, half, rows, wide),) * 2,
            in_specs=[vmem()] * 3 + specs,
            out_specs=(vmem(),) * 2,
            compiler_params=PARAMS,
            cost_estimate=BRIEF,
        )(highs[high], lows[low], turned, *arrays)

    def owned(value, high, low, leaves):
        if not leaves and high == low == 0:
            return value
        pairs = []
        for s in range(seq):
            for h in range(groups):
                k = low if (h >= half) == leaves else high
                pairs.append((s * groups + h, (s ^ 2 * k) * groups + (h ^ 2 * leaves)))
        return lax.ppermute(value, ("seq", "head"), pairs)

    sends, keeps, aways, stays, found = {}, {}, {}, {}, {}
    for n, (high, low) in enumerate(chunks):
        sends[n], keeps[n] = projected(high, low, order_of_projection(n, keeps, stays, found))
        came = swap(sends[n], 0, 1)
        specs, arrays = after(*order_of_split(n, found))
        aways[n], stays[n] = pl.pallas_call(
            split_kernel,
            out_shape=(shaped(2, rows, wide),) * 2,
            in_specs=[vmem()] * 2 + specs,
            out_specs=(vmem(),) * 2,
            compiler_params=PARAMS,
        )(came, keeps[n], *arrays)
        found[n] = (owned(aways[n], high, low, True), owned(stays[n], high, low, False))
    flat = wide % 128 == 0
    joined = pl.pallas_call(
        functools.partial(join_kernel, chunks),
        out_shape=jax.ShapeDtypeStruct((rows, seq * wide) if flat else (chips, 2, rows, wide), BF16),
        in_specs=[vmem()] * (2 * chips),
        out_specs=vmem(),
        compiler_params=PARAMS,
    )(*[piece for n in range(chips) for piece in found[n]])
    return joined if flat else joined.transpose(2, 0, 1, 3).reshape(rows, seq * wide)


def solution(mesh):
    placed = (
        P("seq", "head"),
        P("seq", "head"),
        P("seq", "head"),
        P("head"),
        P("seq", None),
        P("seq", "head"),
    )
    return jax.shard_map(
        local, mesh=mesh, in_specs=placed, out_specs=P(("seq", "head"), None), check_vma=False
    )
```

```python
import functools
import math

import jax
import jax.numpy as jnp
from jax import lax
from jax.experimental import pallas as pl
from jax.experimental.pallas import tpu as pltpu
from jax.sharding import PartitionSpec as P

BLOCK = 128
HALO = 64
NEGATIVE_FILL = -1e30
LAST = (((1,), (1,)), ((), ()))
BF16 = jnp.bfloat16
PARAMS = pltpu.CompilerParams(vmem_limit_bytes=32 << 20)


def vmem():
    return pl.BlockSpec(memory_space=pltpu.VMEM)


def smem():
    return pl.BlockSpec(memory_space=pltpu.SMEM)


def hbm():
    return pl.BlockSpec(memory_space=pltpu.HBM)


def shaped(*shape):
    return pltpu.VMEM(shape, BF16)


def far_away(*arrays):
    return [pltpu.with_memory_space_constraint(array, pltpu.HBM) for array in arrays]


def column_of(count, width, number):
    row = lax.broadcasted_iota(jnp.int32, (count, width), 0)
    found = jnp.zeros((count, width), jnp.int32)
    for r in range(count):
        found = jnp.where(row == r, number(r), found)
    return found


def pick_kernel(
    picks_ref, band_ref, q_hbm, k_hbm, v_hbm, summary_ref, halo_ref, width_ref, q_ref, k_ref, v_ref, sems
):
    per_block = picks_ref.shape[1]
    copies = [
        pltpu.make_async_copy(ref, into, sems.at[part])
        for part, (ref, into) in enumerate(((k_hbm, k_ref), (v_hbm, v_ref), (q_hbm, q_ref)))
    ]
    for copy in copies:
        copy.start()
    wanted = column_of(per_block, BLOCK, lambda r: picks_ref[0, r])
    width_ref[...] = column_of(*width_ref.shape, lambda r: band_ref[r])
    column = lax.broadcasted_iota(jnp.int32, (per_block, BLOCK), 1)
    chosen = jnp.where(column == wanted, 1.0, 0.0).astype(BF16)
    for part, ref in enumerate((k_ref, v_ref)):
        copies[part].wait()
        taken = jnp.dot(chosen, ref[...], preferred_element_type=jnp.float32)
        summary_ref[part] = taken.astype(BF16)
        halo_ref[part] = ref[BLOCK - HALO :, :]
    copies[2].wait()


def stack_kernel(*refs):
    for k, ref in enumerate(refs[:-1]):
        refs[-1][k] = ref[...]


def attend_kernel(low, width_ref, q_ref, k_ref, v_ref, *refs):
    halo_ref, mine_ref, other_ref = (refs if low else (None,) + refs)[:3]
    out_ref = refs[-1]
    size = BLOCK
    heads = q_ref.shape[1] // size
    start, count = (0, HALO) if low else (HALO, BLOCK - HALO)
    reach = start + count
    chips, unused, per_block, unused = mine_ref.shape
    far_rows = chips * per_block
    place = lax.axis_index("seq")
    chip = place // 2
    core = lax.rem(place, 2)
    scale = 1.0 / math.sqrt(size)
    never = 4 * BLOCK

    def distance(columns):
        row = lax.broadcasted_iota(jnp.int32, (count, columns), 0) + start
        return row - lax.broadcasted_iota(jnp.int32, (count, columns), 1)

    gap = distance(reach)
    gaps = [jnp.where(gap >= 0, gap, never)]
    if low:
        gaps.append(jnp.where(place > 0, distance(HALO) + HALO, never))
    far_chip = (lax.broadcasted_iota(jnp.int32, (count, far_rows), 1) // per_block) ^ chip
    gaps.append(jnp.where(far_chip * 2 + core < place, 0, never))
    gaps.append(jnp.where(far_chip * 2 + (1 - core) < place, 0, never))
    gap = jnp.concatenate(gaps, 1)
    listed = gap.shape[1]
    some = 2 if heads % 2 == 0 else 1
    starts = range(0, heads, some)

    def listing(part, own, first):
        cols = slice(first * size, (first + some) * size)
        return jnp.concatenate(
            [own[:reach, cols]]
            + ([halo_ref[part, :, cols]] if low else [])
            + [ref[:, part, :, cols].reshape(far_rows, some * size) for ref in (mine_ref, other_ref)],
            0,
        )

    scores = []
    for first in starts:
        query = q_ref[start:reach, first * size : (first + some) * size]
        if some == 2:
            zero = jnp.zeros((count, size), BF16)
            query = jnp.concatenate(
                [
                    jnp.concatenate([query[:, :size], zero], 1),
                    jnp.concatenate([zero, query[:, size:]], 1),
                ],
                0,
            )
        scores.append(
            lax.dot_general(query, listing(0, k_ref, first), LAST, preferred_element_type=jnp.float32)
        )
    weights, totals = [], []
    for h in range(heads):
        valid = gap < width_ref[h : h + 1, :listed]
        rows = slice(h % some * count, (h % some + 1) * count)
        part = jnp.where(valid, scores[h // some][rows] * scale, NEGATIVE_FILL)
        largest = jnp.max(part, axis=1, keepdims=True)
        part = jnp.where(valid, jnp.exp(part - largest), 0.0)
        totals.append(jnp.sum(part, axis=1, keepdims=True))
        weights.append(part.astype(BF16))
    for first in starts:
        rounded = jnp.concatenate(weights[first : first + some], 0)
        mixed = jnp.dot(rounded, listing(1, v_ref, first), preferred_element_type=jnp.float32)
        for j in range(some):
            taken = mixed[j * count : (j + 1) * count, j * size : (j + 1) * size]
            out_ref[:, (first + j) * size : (first + j + 1) * size] = (taken / totals[first + j]).astype(BF16)


def turn_kernel(mine_hbm, other_ref, order_ref, out_ref, mine_ref, sem):
    core = lax.rem(lax.axis_index("seq"), 2)
    wide = mine_ref.shape[0]
    step = math.gcd(wide, 128)
    copy = pltpu.make_async_copy(mine_hbm, mine_ref, sem)
    copy.start()
    for which, ref in ((1 - core, other_ref), (core, mine_ref)):
        if ref is mine_ref:
            copy.wait()
        for n in range(0, wide, step):
            out_ref[which, :, n : n + step] = ref[n : n + step, :].T


def project_kernel(high_ref, low_ref, turned_ref, *refs):
    send_ref, keep_ref = refs[-2:]
    side = lax.rem(lax.axis_index("head"), 2)
    rows_in = [ref[part] for part in (1 - side, side) for ref in (high_ref, low_ref)]
    rows_in = jnp.concatenate(rows_in, 0)
    for which in range(2):
        found = jnp.dot(rows_in, turned_ref[which], preferred_element_type=jnp.float32)
        found = found.astype(BF16).reshape((2,) + send_ref.shape[1:])
        send_ref[which] = found[0]
        keep_ref[which] = found[1]


def split_kernel(came_ref, keep_ref, *refs):
    away_ref, stay_ref = refs[-2:]
    side = lax.axis_index("head") // 2
    for ref, which in ((away_ref, side), (stay_ref, 1 - side)):
        total = came_ref[:, which].astype(jnp.float32) + keep_ref[:, which].astype(jnp.float32)
        ref[...] = total.astype(BF16)


def split_both_kernel(first_came, first_keep, came_ref, keep_ref, *refs):
    away_ref, *stay_refs = refs[-3:]
    side = lax.axis_index("head") // 2
    for n, (came, keep) in enumerate(((first_came, first_keep), (came_ref, keep_ref))):
        away = came[:, side].astype(jnp.float32) + keep[:, side].astype(jnp.float32)
        away_ref[n] = away.astype(BF16)
        stay = came[:, 1 - side].astype(jnp.float32) + keep[:, 1 - side].astype(jnp.float32)
        stay_refs[n][...] = stay.astype(BF16)


def add_both_kernel(came_ref, *refs):
    for n in range(2):
        total = came_ref[n].astype(jnp.float32) + refs[n][...].astype(jnp.float32)
        refs[2 + n][...] = total.astype(BF16)


def join_kernel(chunks, *refs):
    out_ref = refs[-1]
    wide = refs[0].shape[-1]
    chip = lax.axis_index("seq") // 2
    upper = lax.axis_index("head") // 2
    at = 0
    for high, low, count in chunks:
        total = refs[at][...]
        if count == 2:
            total = (total.astype(jnp.float32) + refs[at + 1][...].astype(jnp.float32)).astype(BF16)
        at += count
        source = chip ^ (high if high == low else jnp.where(upper == 1, high, low))
        if len(out_ref.shape) == 4:
            out_ref[source] = total
            continue
        for c in range(2):
            start = pl.multiple_of(source * (2 * wide), 128)
            out_ref[:, pl.ds(start + c * wide, wide)] = total[c]


def order_of_projection(n, keeps):
    return [keeps[n - 1]] if 0 < n < 4 else []


def order_of_split(n, stays, found):
    return [found[0][0], stays[2]] if n == 3 else []


def local(queries, keys, values, band, picks, w_out):
    heads = band.shape[0]
    tok_rows, feat = queries.shape
    per_block = picks.shape[1]
    seq = lax.axis_size("seq")
    groups = lax.axis_size("head")
    wide = w_out.shape[0]
    rows = tok_rows // groups
    chips = seq // 2
    half = groups // 2

    def swap(value, k, z):
        if k == 0:
            return lax.ppermute(value, "head", [(i, i ^ z) for i in range(groups)])
        if z == 0:
            return lax.ppermute(value, "seq", [(i, i ^ k) for i in range(seq)])
        pairs = [
            (s * groups + h, (s ^ k) * groups + (h ^ z)) for s in range(seq) for h in range(groups)
        ]
        return lax.ppermute(value, ("seq", "head"), pairs)

    other_w = swap(w_out, 1, 0)
    listed = BLOCK + seq * per_block
    summary, halo, width, queries, keys, values = pl.pallas_call(
        pick_kernel,
        out_shape=(
            shaped(2, per_block, feat),
            shaped(2, HALO, feat),
            pltpu.VMEM((heads, listed), jnp.int32),
        )
        + (shaped(tok_rows, feat),) * 3,
        in_specs=[smem(), smem(), hbm(), hbm(), hbm()],
        out_specs=(vmem(),) * 6,
        scratch_shapes=[pltpu.SemaphoreType.DMA((3,))],
        compiler_params=PARAMS,
    )(*far_away(picks, band, queries, keys, values))
    far = [summary] + [swap(summary, 2 * k, 0) for k in range(1, chips)]
    halo = lax.ppermute(halo, "seq", [(i, i + 1) for i in range(seq - 1)])
    mine = pl.pallas_call(
        stack_kernel,
        out_shape=shaped(chips, 2, per_block, feat),
        in_specs=[vmem()] * chips,
        out_specs=vmem(),
        compiler_params=PARAMS,
    )(*far)
    other = swap(mine, 1, 0)
    turned = pl.pallas_call(
        turn_kernel,
        out_shape=shaped(2, feat, wide),
        in_specs=[hbm(), vmem(), pl.BlockSpec(memory_space=pl.ANY)],
        out_specs=vmem(),
        scratch_shapes=[pltpu.VMEM((wide, feat), BF16), pltpu.SemaphoreType.DMA(())],
        compiler_params=PARAMS,
    )(*far_away(w_out), other_w, mine)

    def attended(low, behind, order=()):
        return pl.pallas_call(
            functools.partial(attend_kernel, low),
            out_shape=shaped(HALO if low else tok_rows - HALO, feat),
            in_specs=[vmem()] * (6 + len(behind)) + [pl.BlockSpec(memory_space=pl.ANY)] * len(order),
            out_specs=vmem(),
            compiler_params=PARAMS,
        )(width, queries, keys, values, *behind, mine, other, *order).reshape(half, rows, feat)

    highs = [attended(False, (), (halo, turned,))]
    lows = [attended(True, (halo,), (turned,))]
    for k in range(1, chips):
        if k == 3:
            highs.append(swap(highs[1], 4, 0))
            lows.append(swap(lows[2], 2, 0))
            continue
        highs.append(swap(highs[0], 2 * k, 0))
        lows.append(swap(lows[0], 2 * k, 0))
    chunks = [(0, 0)] + [(1, 2), (2, 1)][: 2 if chips > 2 else 0] + ([(1, 1)] if chips == 2 else [])
    chunks += [(k, k) for k in range(3, chips)]

    def after(*arrays):
        return [pl.BlockSpec(memory_space=pl.ANY)] * len(arrays), arrays

    def projected(high, low, order):
        specs, arrays = after(*order)
        return pl.pallas_call(
            project_kernel,
            out_shape=(shaped(2, half, rows, wide),) * 2,
            in_specs=[vmem()] * 3 + specs,
            out_specs=(vmem(),) * 2,
            compiler_params=PARAMS,
        )(highs[high], lows[low], turned, *arrays)

    def owned(value, high, low, leaves):
        if not leaves and high == low == 0:
            return value
        pairs = []
        for s in range(seq):
            for h in range(groups):
                k = low if (h >= half) == leaves else high
                pairs.append((s * groups + h, (s ^ 2 * k) * groups + (h ^ 2 * leaves)))
        return lax.ppermute(value, ("seq", "head"), pairs)

    sends, keeps, cames, aways, stays, found = {}, {}, {}, {}, {}, {}
    for n, (high, low) in enumerate(chunks):
        sends[n], keeps[n] = projected(high, low, order_of_projection(n, keeps))
        cames[n] = swap(sends[n], 0, 1)
        if n == 0 and chips > 1:
            continue
        specs, arrays = after(*order_of_split(n, stays, found))
        if n == 1:
            away, stays[0], stays[1] = pl.pallas_call(
                split_both_kernel,
                out_shape=(shaped(2, 2, rows, wide),) + (shaped(2, rows, wide),) * 2,
                in_specs=[vmem()] * 4 + specs,
                out_specs=(vmem(),) * 3,
                compiler_params=PARAMS,
            )(cames[0], keeps[0], cames[1], keeps[1], *arrays)
            totals = pl.pallas_call(
                add_both_kernel,
                out_shape=(shaped(2, rows, wide),) * 2,
                in_specs=[vmem()] * 3,
                out_specs=(vmem(),) * 2,
                compiler_params=PARAMS,
            )(swap(away, 0, 2), stays[0], stays[1])
            found[0], found[1] = [totals[0]], [owned(totals[1], high, low, False)]
            continue
        aways[n], stays[n] = pl.pallas_call(
            split_kernel,
            out_shape=(shaped(2, rows, wide),) * 2,
            in_specs=[vmem()] * 2 + specs,
            out_specs=(vmem(),) * 2,
            compiler_params=PARAMS,
        )(cames[n], keeps[n], *arrays)
        found[n] = [owned(aways[n], high, low, True), owned(stays[n], high, low, False)]
    flat = wide % 128 == 0
    joined = pl.pallas_call(
        functools.partial(
            join_kernel, [(high, low, len(found[n])) for n, (high, low) in enumerate(chunks)]
        ),
        out_shape=jax.ShapeDtypeStruct((rows, seq * wide) if flat else (chips, 2, rows, wide), BF16),
        in_specs=[vmem()] * sum(len(pieces) for pieces in found.values()),
        out_specs=vmem(),
        compiler_params=PARAMS,
    )(*[piece for n in range(chips) for piece in found[n]])
    return joined if flat else joined.transpose(2, 0, 1, 3).reshape(rows, seq * wide)


def solution(mesh):
    placed = (
        P("seq", "head"),
        P("seq", "head"),
        P("seq", "head"),
        P("head"),
        P("seq", None),
        P("seq", "head"),
    )
    return jax.shard_map(
        local, mesh=mesh, in_specs=placed, out_specs=P(("seq", "head"), None), check_vma=False
    )
```

```python
import functools
import math

import jax
import jax.numpy as jnp
from jax import lax
from jax.experimental import pallas as pl
from jax.experimental.pallas import tpu as pltpu
from jax.sharding import PartitionSpec as P

BLOCK = 128
HALO = 64
NEGATIVE_FILL = -1e30
LAST = (((1,), (1,)), ((), ()))
BF16 = jnp.bfloat16
BRIEF = pl.CostEstimate(flops=0, bytes_accessed=0, transcendentals=0)
LONGER = pl.CostEstimate(flops=1_100_000_000, bytes_accessed=3_000_000, transcendentals=0)
PARAMS = pltpu.CompilerParams(vmem_limit_bytes=32 << 20)


def vmem():
    return pl.BlockSpec(memory_space=pltpu.VMEM)


def smem():
    return pl.BlockSpec(memory_space=pltpu.SMEM)


def hbm():
    return pl.BlockSpec(memory_space=pltpu.HBM)


def shaped(*shape):
    return pltpu.VMEM(shape, BF16)


def far_away(*arrays):
    return [pltpu.with_memory_space_constraint(array, pltpu.HBM) for array in arrays]


def column_of(count, width, number):
    row = lax.broadcasted_iota(jnp.int32, (count, width), 0)
    found = jnp.zeros((count, width), jnp.int32)
    for r in range(count):
        found = jnp.where(row == r, number(r), found)
    return found


def pick_kernel(
    picks_ref, band_ref, q_hbm, k_hbm, v_hbm, summary_ref, halo_ref, width_ref, q_ref, k_ref, v_ref, sems
):
    per_block = picks_ref.shape[1]
    copies = [
        pltpu.make_async_copy(ref, into, sems.at[part])
        for part, (ref, into) in enumerate(((k_hbm, k_ref), (v_hbm, v_ref), (q_hbm, q_ref)))
    ]
    for copy in copies:
        copy.start()
    wanted = column_of(per_block, BLOCK, lambda r: picks_ref[0, r])
    width_ref[...] = column_of(*width_ref.shape, lambda r: band_ref[r])
    column = lax.broadcasted_iota(jnp.int32, (per_block, BLOCK), 1)
    chosen = jnp.where(column == wanted, 1.0, 0.0).astype(BF16)
    for part, ref in enumerate((k_ref, v_ref)):
        copies[part].wait()
        taken = jnp.dot(chosen, ref[...], preferred_element_type=jnp.float32)
        summary_ref[part] = taken.astype(BF16)
        halo_ref[part] = ref[BLOCK - HALO :, :]
    copies[2].wait()


def stack_kernel(*refs):
    for k, ref in enumerate(refs[:-1]):
        refs[-1][k] = ref[...]


def attend_kernel(low, width_ref, q_ref, k_ref, v_ref, *refs):
    halo_ref, mine_ref, other_ref = (refs if low else (None,) + refs)[:3]
    out_ref = refs[-1]
    size = BLOCK
    heads = q_ref.shape[1] // size
    start, count = (0, HALO) if low else (HALO, BLOCK - HALO)
    reach = start + count
    chips, unused, per_block, unused = mine_ref.shape
    far_rows = chips * per_block
    place = lax.axis_index("seq")
    chip = place // 2
    core = lax.rem(place, 2)
    scale = 1.0 / math.sqrt(size)
    never = 4 * BLOCK

    def distance(columns):
        row = lax.broadcasted_iota(jnp.int32, (count, columns), 0) + start
        return row - lax.broadcasted_iota(jnp.int32, (count, columns), 1)

    gap = distance(reach)
    gaps = [jnp.where(gap >= 0, gap, never)]
    if low:
        gaps.append(jnp.where(place > 0, distance(HALO) + HALO, never))
    far_chip = (lax.broadcasted_iota(jnp.int32, (count, far_rows), 1) // per_block) ^ chip
    gaps.append(jnp.where(far_chip * 2 + core < place, 0, never))
    gaps.append(jnp.where(far_chip * 2 + (1 - core) < place, 0, never))
    gap = jnp.concatenate(gaps, 1)
    listed = gap.shape[1]
    some = 2 if heads % 2 == 0 else 1
    starts = range(0, heads, some)

    def listing(part, own, first):
        cols = slice(first * size, (first + some) * size)
        return jnp.concatenate(
            [own[:reach, cols]]
            + ([halo_ref[part, :, cols]] if low else [])
            + [ref[:, part, :, cols].reshape(far_rows, some * size) for ref in (mine_ref, other_ref)],
            0,
        )

    scores = []
    for first in starts:
        query = q_ref[start:reach, first * size : (first + some) * size]
        if some == 2:
            zero = jnp.zeros((count, size), BF16)
            query = jnp.concatenate(
                [
                    jnp.concatenate([query[:, :size], zero], 1),
                    jnp.concatenate([zero, query[:, size:]], 1),
                ],
                0,
            )
        scores.append(
            lax.dot_general(query, listing(0, k_ref, first), LAST, preferred_element_type=jnp.float32)
        )
    weights, totals = [], []
    for h in range(heads):
        valid = gap < width_ref[h : h + 1, :listed]
        rows = slice(h % some * count, (h % some + 1) * count)
        part = jnp.where(valid, scores[h // some][rows] * scale, NEGATIVE_FILL)
        largest = jnp.max(part, axis=1, keepdims=True)
        part = jnp.where(valid, jnp.exp(part - largest), 0.0)
        totals.append(jnp.sum(part, axis=1, keepdims=True))
        weights.append(part.astype(BF16))
    for first in starts:
        rounded = jnp.concatenate(weights[first : first + some], 0)
        mixed = jnp.dot(rounded, listing(1, v_ref, first), preferred_element_type=jnp.float32)
        for j in range(some):
            taken = mixed[j * count : (j + 1) * count, j * size : (j + 1) * size]
            out_ref[:, (first + j) * size : (first + j + 1) * size] = (taken / totals[first + j]).astype(BF16)


def turn_kernel(mine_hbm, other_ref, order_ref, out_ref, mine_ref, sem):
    core = lax.rem(lax.axis_index("seq"), 2)
    wide = mine_ref.shape[0]
    step = math.gcd(wide, 128)
    copy = pltpu.make_async_copy(mine_hbm, mine_ref, sem)
    copy.start()
    for which, ref in ((1 - core, other_ref), (core, mine_ref)):
        if ref is mine_ref:
            copy.wait()
        for n in range(0, wide, step):
            out_ref[which, :, n : n + step] = ref[n : n + step, :].T


def project_kernel(high_ref, low_ref, turned_ref, *refs):
    send_ref, keep_ref = refs[-2:]
    side = lax.rem(lax.axis_index("head"), 2)
    rows_in = [ref[part] for part in (1 - side, side) for ref in (high_ref, low_ref)]
    rows_in = jnp.concatenate(rows_in, 0)
    for which in range(2):
        found = jnp.dot(rows_in, turned_ref[which], preferred_element_type=jnp.float32)
        found = found.astype(BF16).reshape((2,) + send_ref.shape[1:])
        send_ref[which] = found[0]
        keep_ref[which] = found[1]


def split_kernel(came_ref, keep_ref, *refs):
    away_ref, stay_ref = refs[-2:]
    side = lax.axis_index("head") // 2
    for ref, which in ((away_ref, side), (stay_ref, 1 - side)):
        total = came_ref[:, which].astype(jnp.float32) + keep_ref[:, which].astype(jnp.float32)
        ref[...] = total.astype(BF16)


def join_kernel(chunks, *refs):
    out_ref = refs[-1]
    wide = refs[0].shape[-1]
    chip = lax.axis_index("seq") // 2
    upper = lax.axis_index("head") // 2
    for n, (high, low) in enumerate(chunks):
        total = refs[2 * n][...].astype(jnp.float32) + refs[2 * n + 1][...].astype(jnp.float32)
        total = total.astype(BF16)
        source = chip ^ (high if high == low else jnp.where(upper == 1, high, low))
        if len(out_ref.shape) == 4:
            out_ref[source] = total
            continue
        for c in range(2):
            start = pl.multiple_of(source * (2 * wide), 128)
            out_ref[:, pl.ds(start + c * wide, wide)] = total[c]


def order_of_projection(n, keeps, stays, found):
    if n == 3:
        return [keeps[2], stays[1], found[0][0]]
    return [keeps[n - 1]] if 0 < n < 3 else []


def order_of_split(n, found):
    return [found[1][0]] if n == 3 else []


def local(queries, keys, values, band, picks, w_out):
    heads = band.shape[0]
    tok_rows, feat = queries.shape
    per_block = picks.shape[1]
    seq = lax.axis_size("seq")
    groups = lax.axis_size("head")
    wide = w_out.shape[0]
    rows = tok_rows // groups
    chips = seq // 2
    half = groups // 2

    def swap(value, k, z):
        if k == 0:
            return lax.ppermute(value, "head", [(i, i ^ z) for i in range(groups)])
        if z == 0:
            return lax.ppermute(value, "seq", [(i, i ^ k) for i in range(seq)])
        pairs = [
            (s * groups + h, (s ^ k) * groups + (h ^ z)) for s in range(seq) for h in range(groups)
        ]
        return lax.ppermute(value, ("seq", "head"), pairs)

    other_w = swap(w_out, 1, 0)
    listed = BLOCK + seq * per_block
    summary, halo, width, queries, keys, values = pl.pallas_call(
        pick_kernel,
        out_shape=(
            shaped(2, per_block, feat),
            shaped(2, HALO, feat),
            pltpu.VMEM((heads, listed), jnp.int32),
        )
        + (shaped(tok_rows, feat),) * 3,
        in_specs=[smem(), smem(), hbm(), hbm(), hbm()],
        out_specs=(vmem(),) * 6,
        scratch_shapes=[pltpu.SemaphoreType.DMA((3,))],
        compiler_params=PARAMS,
    )(*far_away(picks, band, queries, keys, values))
    far = [summary] + [swap(summary, 2 * k, 0) for k in range(1, chips)]
    halo = lax.ppermute(halo, "seq", [(i, i + 1) for i in range(seq - 1)])
    mine = pl.pallas_call(
        stack_kernel,
        out_shape=shaped(chips, 2, per_block, feat),
        in_specs=[vmem()] * chips,
        out_specs=vmem(),
        compiler_params=PARAMS,
    )(*far)
    other = swap(mine, 1, 0)
    turned = pl.pallas_call(
        turn_kernel,
        out_shape=shaped(2, feat, wide),
        in_specs=[hbm(), vmem(), pl.BlockSpec(memory_space=pl.ANY)],
        out_specs=vmem(),
        scratch_shapes=[pltpu.VMEM((wide, feat), BF16), pltpu.SemaphoreType.DMA(())],
        compiler_params=PARAMS,
    )(*far_away(w_out), other_w, mine)

    def attended(low, behind, order=()):
        return pl.pallas_call(
            functools.partial(attend_kernel, low),
            out_shape=shaped(HALO if low else tok_rows - HALO, feat),
            in_specs=[vmem()] * (6 + len(behind)) + [pl.BlockSpec(memory_space=pl.ANY)] * len(order),
            out_specs=vmem(),
            compiler_params=PARAMS,
            cost_estimate=LONGER,
        )(width, queries, keys, values, *behind, mine, other, *order).reshape(half, rows, feat)

    highs = [attended(False, (), (halo, turned))]
    lows = [attended(True, (halo,), (turned,))]
    for k in range(1, chips):
        if k == 3:
            highs.append(swap(highs[1], 4, 0))
            lows.append(swap(lows[2], 2, 0))
            continue
        highs.append(swap(highs[0], 2 * k, 0))
        lows.append(swap(lows[0], 2 * k, 0))
    chunks = [(0, 0)] + [(1, 2), (2, 1)][: 2 if chips > 2 else 0] + ([(1, 1)] if chips == 2 else [])
    chunks += [(k, k) for k in range(3, chips)]

    def after(*arrays):
        return [pl.BlockSpec(memory_space=pl.ANY)] * len(arrays), arrays

    def projected(high, low, order):
        specs, arrays = after(*order)
        return pl.pallas_call(
            project_kernel,
            out_shape=(shaped(2, half, rows, wide),) * 2,
            in_specs=[vmem()] * 3 + specs,
            out_specs=(vmem(),) * 2,
            compiler_params=PARAMS,
            cost_estimate=BRIEF,
        )(highs[high], lows[low], turned, *arrays)

    def owned(value, high, low, leaves):
        if not leaves and high == low == 0:
            return value
        pairs = []
        for s in range(seq):
            for h in range(groups):
                k = low if (h >= half) == leaves else high
                pairs.append((s * groups + h, (s ^ 2 * k) * groups + (h ^ 2 * leaves)))
        return lax.ppermute(value, ("seq", "head"), pairs)

    sends, keeps, aways, stays, found = {}, {}, {}, {}, {}
    for n, (high, low) in enumerate(chunks):
        sends[n], keeps[n] = projected(high, low, order_of_projection(n, keeps, stays, found))
        came = swap(sends[n], 0, 1)
        specs, arrays = after(*order_of_split(n, found))
        aways[n], stays[n] = pl.pallas_call(
            split_kernel,
            out_shape=(shaped(2, rows, wide),) * 2,
            in_specs=[vmem()] * 2 + specs,
            out_specs=(vmem(),) * 2,
            compiler_params=PARAMS,
        )(came, keeps[n], *arrays)
        found[n] = (owned(aways[n], high, low, True), owned(stays[n], high, low, False))
    flat = wide % 128 == 0
    joined = pl.pallas_call(
        functools.partial(join_kernel, chunks),
        out_shape=jax.ShapeDtypeStruct((rows, seq * wide) if flat else (chips, 2, rows, wide), BF16),
        in_specs=[vmem()] * (2 * chips),
        out_specs=vmem(),
        compiler_params=PARAMS,
    )(*[piece for n in range(chips) for piece in found[n]])
    return joined if flat else joined.transpose(2, 0, 1, 3).reshape(rows, seq * wide)


def solution(mesh):
    placed = (
        P("seq", "head"),
        P("seq", "head"),
        P("seq", "head"),
        P("head"),
        P("seq", None),
        P("seq", "head"),
    )
    return jax.shard_map(
        local, mesh=mesh, in_specs=placed, out_specs=P(("seq", "head"), None), check_vma=False
    )
```

```python
import functools
import math

import jax
import jax.numpy as jnp
from jax import lax
from jax.experimental import pallas as pl
from jax.experimental.pallas import tpu as pltpu
from jax.sharding import PartitionSpec as P

BLOCK = 128
HALO = 64
NEGATIVE_FILL = -1e30
LAST = (((1,), (1,)), ((), ()))
BF16 = jnp.bfloat16
BRIEF = pl.CostEstimate(flops=0, bytes_accessed=0, transcendentals=0)
LONGER = pl.CostEstimate(flops=1_100_000_000, bytes_accessed=3_000_000, transcendentals=0)
PARAMS = pltpu.CompilerParams(vmem_limit_bytes=32 << 20)


def vmem():
    return pl.BlockSpec(memory_space=pltpu.VMEM)


def smem():
    return pl.BlockSpec(memory_space=pltpu.SMEM)


def hbm():
    return pl.BlockSpec(memory_space=pltpu.HBM)


def shaped(*shape):
    return pltpu.VMEM(shape, BF16)


def far_away(*arrays):
    return [pltpu.with_memory_space_constraint(array, pltpu.HBM) for array in arrays]


def column_of(count, width, number):
    row = lax.broadcasted_iota(jnp.int32, (count, width), 0)
    found = jnp.zeros((count, width), jnp.int32)
    for r in range(count):
        found = jnp.where(row == r, number(r), found)
    return found


def pick_kernel(
    picks_ref, band_ref, q_hbm, k_hbm, v_hbm, summary_ref, halo_ref, width_ref, q_ref, k_ref, v_ref, sems
):
    per_block = picks_ref.shape[1]
    copies = [
        pltpu.make_async_copy(ref, into, sems.at[part])
        for part, (ref, into) in enumerate(((k_hbm, k_ref), (v_hbm, v_ref), (q_hbm, q_ref)))
    ]
    for copy in copies:
        copy.start()
    wanted = column_of(per_block, BLOCK, lambda r: picks_ref[0, r])
    width_ref[...] = column_of(*width_ref.shape, lambda r: band_ref[r])
    column = lax.broadcasted_iota(jnp.int32, (per_block, BLOCK), 1)
    chosen = jnp.where(column == wanted, 1.0, 0.0).astype(BF16)
    for part, ref in enumerate((k_ref, v_ref)):
        copies[part].wait()
        taken = jnp.dot(chosen, ref[...], preferred_element_type=jnp.float32)
        summary_ref[part] = taken.astype(BF16)
        halo_ref[part] = ref[BLOCK - HALO :, :]
    copies[2].wait()


def stack_kernel(*refs):
    for k, ref in enumerate(refs[:-1]):
        refs[-1][k] = ref[...]


def attend_kernel(low, width_ref, q_ref, k_ref, v_ref, *refs):
    halo_ref, mine_ref, other_ref = (refs if low else (None,) + refs)[:3]
    out_ref = refs[-1]
    size = BLOCK
    heads = q_ref.shape[1] // size
    start, count = (0, HALO) if low else (HALO, BLOCK - HALO)
    reach = start + count
    chips, unused, per_block, unused = mine_ref.shape
    far_rows = chips * per_block
    place = lax.axis_index("seq")
    chip = place // 2
    core = lax.rem(place, 2)
    scale = 1.0 / math.sqrt(size)
    never = 4 * BLOCK

    def distance(columns):
        row = lax.broadcasted_iota(jnp.int32, (count, columns), 0) + start
        return row - lax.broadcasted_iota(jnp.int32, (count, columns), 1)

    gap = distance(reach)
    gaps = [jnp.where(gap >= 0, gap, never)]
    if low:
        gaps.append(jnp.where(place > 0, distance(HALO) + HALO, never))
    far_chip = (lax.broadcasted_iota(jnp.int32, (count, far_rows), 1) // per_block) ^ chip
    gaps.append(jnp.where(far_chip * 2 + core < place, 0, never))
    gaps.append(jnp.where(far_chip * 2 + (1 - core) < place, 0, never))
    gap = jnp.concatenate(gaps, 1)
    listed = gap.shape[1]
    some = 2 if heads % 2 == 0 else 1
    starts = range(0, heads, some)

    def listing(part, own, first):
        cols = slice(first * size, (first + some) * size)
        return jnp.concatenate(
            [own[:reach, cols]]
            + ([halo_ref[part, :, cols]] if low else [])
            + [ref[:, part, :, cols].reshape(far_rows, some * size) for ref in (mine_ref, other_ref)],
            0,
        )

    scores = []
    for first in starts:
        query = q_ref[start:reach, first * size : (first + some) * size]
        if some == 2:
            zero = jnp.zeros((count, size), BF16)
            query = jnp.concatenate(
                [
                    jnp.concatenate([query[:, :size], zero], 1),
                    jnp.concatenate([zero, query[:, size:]], 1),
                ],
                0,
            )
        scores.append(
            lax.dot_general(query, listing(0, k_ref, first), LAST, preferred_element_type=jnp.float32)
        )
    weights, totals = [], []
    for h in range(heads):
        valid = gap < width_ref[h : h + 1, :listed]
        rows = slice(h % some * count, (h % some + 1) * count)
        part = jnp.where(valid, scores[h // some][rows] * scale, NEGATIVE_FILL)
        largest = jnp.max(part, axis=1, keepdims=True)
        part = jnp.where(valid, jnp.exp(part - largest), 0.0)
        totals.append(jnp.sum(part, axis=1, keepdims=True))
        weights.append(part.astype(BF16))
    for first in starts:
        rounded = jnp.concatenate(weights[first : first + some], 0)
        mixed = jnp.dot(rounded, listing(1, v_ref, first), preferred_element_type=jnp.float32)
        for j in range(some):
            taken = mixed[j * count : (j + 1) * count, j * size : (j + 1) * size]
            out_ref[:, (first + j) * size : (first + j + 1) * size] = (taken / totals[first + j]).astype(BF16)


def turn_kernel(mine_hbm, other_ref, order_ref, out_ref, mine_ref, sem):
    core = lax.rem(lax.axis_index("seq"), 2)
    wide = mine_ref.shape[0]
    step = math.gcd(wide, 128)
    copy = pltpu.make_async_copy(mine_hbm, mine_ref, sem)
    copy.start()
    for which, ref in ((1 - core, other_ref), (core, mine_ref)):
        if ref is mine_ref:
            copy.wait()
        for n in range(0, wide, step):
            out_ref[which, :, n : n + step] = ref[n : n + step, :].T


def project_kernel(high_ref, low_ref, turned_ref, *refs):
    send_ref, keep_ref = refs[-2:]
    side = lax.rem(lax.axis_index("head"), 2)
    rows_in = [ref[part] for part in (1 - side, side) for ref in (high_ref, low_ref)]
    rows_in = jnp.concatenate(rows_in, 0)
    for which in range(2):
        found = jnp.dot(rows_in, turned_ref[which], preferred_element_type=jnp.float32)
        found = found.astype(BF16).reshape((2,) + send_ref.shape[1:])
        send_ref[which] = found[0]
        keep_ref[which] = found[1]


def split_kernel(came_ref, keep_ref, *refs):
    away_ref, stay_ref = refs[-2:]
    side = lax.axis_index("head") // 2
    for ref, which in ((away_ref, side), (stay_ref, 1 - side)):
        total = came_ref[:, which].astype(jnp.float32) + keep_ref[:, which].astype(jnp.float32)
        ref[...] = total.astype(BF16)


def hand_on_kernel(stay_ref, order_ref, out_ref):
    out_ref[...] = stay_ref[...]


def join_kernel(chunks, *refs):
    out_ref = refs[-1]
    wide = refs[0].shape[-1]
    chip = lax.axis_index("seq") // 2
    upper = lax.axis_index("head") // 2
    for n, (high, low) in enumerate(chunks):
        total = refs[2 * n][...].astype(jnp.float32) + refs[2 * n + 1][...].astype(jnp.float32)
        total = total.astype(BF16)
        source = chip ^ (high if high == low else jnp.where(upper == 1, high, low))
        if len(out_ref.shape) == 4:
            out_ref[source] = total
            continue
        for c in range(2):
            start = pl.multiple_of(source * (2 * wide), 128)
            out_ref[:, pl.ds(start + c * wide, wide)] = total[c]


def order_of_projection(n, keeps, stays, found):
    if n == 3:
        return [keeps[2], stays[1], found[0][0]]
    return [keeps[n - 1]] if 0 < n < 3 else []


def order_of_split(n, found):
    return [found[1][0]] if n == 3 else []


def local(queries, keys, values, band, picks, w_out):
    heads = band.shape[0]
    tok_rows, feat = queries.shape
    per_block = picks.shape[1]
    seq = lax.axis_size("seq")
    groups = lax.axis_size("head")
    wide = w_out.shape[0]
    rows = tok_rows // groups
    chips = seq // 2
    half = groups // 2

    def swap(value, k, z):
        if k == 0:
            return lax.ppermute(value, "head", [(i, i ^ z) for i in range(groups)])
        if z == 0:
            return lax.ppermute(value, "seq", [(i, i ^ k) for i in range(seq)])
        pairs = [
            (s * groups + h, (s ^ k) * groups + (h ^ z)) for s in range(seq) for h in range(groups)
        ]
        return lax.ppermute(value, ("seq", "head"), pairs)

    other_w = swap(w_out, 1, 0)
    listed = BLOCK + seq * per_block
    summary, halo, width, queries, keys, values = pl.pallas_call(
        pick_kernel,
        out_shape=(
            shaped(2, per_block, feat),
            shaped(2, HALO, feat),
            pltpu.VMEM((heads, listed), jnp.int32),
        )
        + (shaped(tok_rows, feat),) * 3,
        in_specs=[smem(), smem(), hbm(), hbm(), hbm()],
        out_specs=(vmem(),) * 6,
        scratch_shapes=[pltpu.SemaphoreType.DMA((3,))],
        compiler_params=PARAMS,
    )(*far_away(picks, band, queries, keys, values))
    far = [summary] + [swap(summary, 2 * k, 0) for k in range(1, chips)]
    halo = lax.ppermute(halo, "seq", [(i, i + 1) for i in range(seq - 1)])
    mine = pl.pallas_call(
        stack_kernel,
        out_shape=shaped(chips, 2, per_block, feat),
        in_specs=[vmem()] * chips,
        out_specs=vmem(),
        compiler_params=PARAMS,
    )(*far)
    other = swap(mine, 1, 0)
    turned = pl.pallas_call(
        turn_kernel,
        out_shape=shaped(2, feat, wide),
        in_specs=[hbm(), vmem(), pl.BlockSpec(memory_space=pl.ANY)],
        out_specs=vmem(),
        scratch_shapes=[pltpu.VMEM((wide, feat), BF16), pltpu.SemaphoreType.DMA(())],
        compiler_params=PARAMS,
    )(*far_away(w_out), other_w, mine)

    def attended(low, behind, order=()):
        return pl.pallas_call(
            functools.partial(attend_kernel, low),
            out_shape=shaped(HALO if low else tok_rows - HALO, feat),
            in_specs=[vmem()] * (6 + len(behind)) + [pl.BlockSpec(memory_space=pl.ANY)] * len(order),
            out_specs=vmem(),
            compiler_params=PARAMS,
            cost_estimate=LONGER,
        )(width, queries, keys, values, *behind, mine, other, *order).reshape(half, rows, feat)

    highs = [attended(False, (), (halo, turned))]
    lows = [attended(True, (halo,), (turned,))]
    for k in range(1, chips):
        if k == 3:
            highs.append(swap(highs[1], 4, 0))
            lows.append(swap(lows[2], 2, 0))
            continue
        highs.append(swap(highs[0], 2 * k, 0))
        lows.append(swap(lows[0], 2 * k, 0))
    chunks = [(0, 0)] + [(1, 2), (2, 1)][: 2 if chips > 2 else 0] + ([(1, 1)] if chips == 2 else [])
    chunks += [(k, k) for k in range(3, chips)]

    def after(*arrays):
        return [pl.BlockSpec(memory_space=pl.ANY)] * len(arrays), arrays

    def projected(high, low, order):
        specs, arrays = after(*order)
        return pl.pallas_call(
            project_kernel,
            out_shape=(shaped(2, half, rows, wide),) * 2,
            in_specs=[vmem()] * 3 + specs,
            out_specs=(vmem(),) * 2,
            compiler_params=PARAMS,
            cost_estimate=BRIEF,
        )(highs[high], lows[low], turned, *arrays)

    def owned(value, high, low, leaves):
        if not leaves and high == low == 0:
            return value
        pairs = []
        for s in range(seq):
            for h in range(groups):
                k = low if (h >= half) == leaves else high
                pairs.append((s * groups + h, (s ^ 2 * k) * groups + (h ^ 2 * leaves)))
        return lax.ppermute(value, ("seq", "head"), pairs)

    sends, keeps, aways, stays, found = {}, {}, {}, {}, {}
    for n, (high, low) in enumerate(chunks):
        sends[n], keeps[n] = projected(high, low, order_of_projection(n, keeps, stays, found))
        came = swap(sends[n], 0, 1)
        specs, arrays = after(*order_of_split(n, found))
        aways[n], stays[n] = pl.pallas_call(
            split_kernel,
            out_shape=(shaped(2, rows, wide),) * 2,
            in_specs=[vmem()] * 2 + specs,
            out_specs=(vmem(),) * 2,
            compiler_params=PARAMS,
        )(came, keeps[n], *arrays)
        found[n] = [owned(aways[n], high, low, True), None]
        if n != 1:
            found[n][1] = owned(stays[n], high, low, False)
        if n == min(2, chips - 1) and chips > 1:
            stay = pl.pallas_call(
                hand_on_kernel,
                out_shape=shaped(2, rows, wide),
                in_specs=[vmem(), pl.BlockSpec(memory_space=pl.ANY)],
                out_specs=vmem(),
                compiler_params=PARAMS,
            )(stays[1], aways[n])
            found[1][1] = owned(stay, *chunks[1], False)
    flat = wide % 128 == 0
    joined = pl.pallas_call(
        functools.partial(join_kernel, chunks),
        out_shape=jax.ShapeDtypeStruct((rows, seq * wide) if flat else (chips, 2, rows, wide), BF16),
        in_specs=[vmem()] * (2 * chips),
        out_specs=vmem(),
        compiler_params=PARAMS,
    )(*[piece for n in range(chips) for piece in found[n]])
    return joined if flat else joined.transpose(2, 0, 1, 3).reshape(rows, seq * wide)


def solution(mesh):
    placed = (
        P("seq", "head"),
        P("seq", "head"),
        P("seq", "head"),
        P("head"),
        P("seq", None),
        P("seq", "head"),
    )
    return jax.shard_map(
        local, mesh=mesh, in_specs=placed, out_specs=P(("seq", "head"), None), check_vma=False
    )
```
